32 devices in a mesh: grp: 4 (over y, x), dev: 8 (over z, core).
Axes of the slice: x: 2, y: 2, z: 4, core: 2. Of those that a mesh axis runs over, the one named last changes fastest.
Arguments:
- rhs: float32 [16, 32768], P(None, ('grp', 'dev')), may hold values from -6 to 6
- leaf_basis: float32 [64, 32768], P(None, ('grp', 'dev'))
- near_blocks: float32 [64, 65536], P(None, ('grp', 'dev')), may hold values from -0.75 to 0.75
- near_partner: int32 [512], P(('grp', 'dev')), may hold values from 0 to 511, as said below
- local_transfer: float32 [64, 61440], P(None, ('grp', 'dev'))
- local_coupling: float32 [64, 61440], P(None, ('grp', 'dev')), may hold values from -0.75 to 0.75
- far_partner: int32 [32, 30], P(('grp', 'dev')), may hold values from 0 to 511, as said below
- dev_transfer: float32 [4, 64, 896], P('grp')
- dev_coupling: float32 [4, 64, 896], P('grp'), may hold values from -4 to 4
- grp_transfer: float32 [64, 384], replicated
- grp_coupling: float32 [64, 384], replicated, may hold values from -6 to 6
Outputs:
- product: float32 [16, 32768], P(None, ('grp', 'dev'))
- root_factor: float32 [64, 64], replicated
The draws below stay inside these ranges and needn't reach their ends.
Inputs may be any that keep to these rules, and one draw needn't show every extreme that they name: near_partner[l] is a leaf other than l, at most 16 leaves away; some leaf's partner is exactly 16 leaves away. `far_partner`: in row s, entry 2 * 16 - 2 * m + j (m = 16 >> k, level k, 0 <= j < m) names a node of level k other than node s * m + j and at most m nodes from it; at every level some entry is exactly m nodes away.
All inputs are finite; a program needn't handle non-finite values.
Results may differ from the reference program's by a relative error of at most 0.0001.
Values sent between devices are 32-bit elements; how exact they have to be, the bound alone decides.
No kernel may reach another device: no remote copies, remote signals or barrier semaphores. Data moves between devices by JAX's collectives and lax.ppermute only.
A program may use at most 64 MiB of HBM per device.

```python
import math
import jax
import jax.numpy as jnp
from jax import lax

RANK = 64
LEAF = 64
NRHS = 16
LOC = 4
LEAF_DEV = 16
LOG_DEV = 3
LOG_GRP = 2
GROUPS = 4
SUBTREES = 32
LEAVES = 512
UNKNOWNS = 32768
LOCAL_NODES = 30
DEV_NODES = 14
GRP_NODES = 6
N_GRP = 4
N_DEV = 8


def spread_partner(key, node_count, reach_nodes):
    first_key, second_key, third_key = jax.random.split(key, 3)
    distance = jax.random.randint(first_key, (node_count,), 1, reach_nodes + 1)
    longest = jax.random.randint(second_key, (), 0, node_count)
    node_ids = jnp.arange(node_count)
    distance = jnp.where(node_ids == longest, reach_nodes, distance)
    direction = 2 * jax.random.randint(third_key, (node_count,), 0, 2) - 1
    forward = node_ids + direction * distance
    backward = node_ids - direction * distance
    inside = (forward >= 0) & (forward < node_count)
    return jnp.where(inside, forward, backward).astype(jnp.int32)


def near_identity(key, leading, row_count, block_width, block_count, scale):
    array_shape = leading + (row_count, block_count * block_width)
    noise_part = jax.random.normal(key, array_shape, jnp.float32)
    diagonal = (jnp.arange(row_count)[:, None] == jnp.arange(block_count * block_width)[None, :] % block_width).astype(jnp.float32)
    return scale * (diagonal + 0.35 / math.sqrt(block_width) * noise_part)


def draw_leaf_basis(key, part):
    basis = near_identity(jax.random.fold_in(key, 3), (), LEAF, RANK, LEAVES, 1.0)
    return basis


def draw_near_partner(key, part):
    return spread_partner(jax.random.fold_in(key, 11), LEAVES, LEAF_DEV)


def draw_far_partner(key, part):
    columns = []
    for tree_level in range(LOC):
        level_nodes = LEAF_DEV >> tree_level
        chosen = spread_partner(jax.random.fold_in(key, 100 + tree_level), SUBTREES * level_nodes, level_nodes)
        columns.append(chosen.reshape(SUBTREES, level_nodes))
    return jnp.concatenate(columns, axis=1)


def draw_local_transfer(key, part):
    return near_identity(jax.random.fold_in(key, 21), (), RANK, RANK, SUBTREES * LOCAL_NODES, 0.70710678)


def draw_dev_transfer(key, part):
    return near_identity(jax.random.fold_in(key, 31), (GROUPS,), RANK, RANK, DEV_NODES, 0.70710678)


def draw_grp_transfer(key, part):
    return near_identity(jax.random.fold_in(key, 41), (), RANK, RANK, GRP_NODES, 0.70710678)


def block_levels(stream_key, dims, shards, smallest, largest):
    def one(axis_at, parts):
        draws = jax.random.uniform(jax.random.fold_in(jax.random.fold_in(stream_key, 6), axis_at), (parts,), jnp.float32, smallest / len(shards), largest / len(shards))
        return jnp.repeat(jnp.exp(draws), dims[axis_at] // parts).reshape((-1,) + (1,) * (len(dims) - axis_at - 1))

    loudness = one(*shards[0])
    for cut in shards[1:]:
        loudness = loudness * one(*cut)
    return loudness


def gaussian(stream_key, shape, width, limit, cuts=(), kind=jnp.bfloat16):
    array = jax.random.normal(stream_key, shape, jnp.float32) * width
    if len(cuts) > 0:
        array = block_levels(stream_key, shape, cuts, -0.22, 0.18) * array
    return jnp.clip(array, min=-limit, max=limit).astype(kind)


def setup_inputs(seed: int = 0) -> dict:
    seeds = jax.random.split(jax.random.key(seed), 12)
    return {
        "rhs": gaussian(seeds[0], (NRHS, UNKNOWNS), 1.0, 6.0, ((1, 32),), jnp.float32),
        "leaf_basis": draw_leaf_basis(jax.random.fold_in(seeds[11], 71), 0),
        "near_blocks": gaussian(seeds[2], (LEAF, 2 * LEAVES * LEAF), LEAF ** -0.5, 0.75, ((1, 32),), jnp.float32),
        "near_partner": draw_near_partner(jax.random.fold_in(seeds[11], 71), 0),
        "local_transfer": draw_local_transfer(jax.random.fold_in(seeds[11], 71), 0),
        "local_coupling": gaussian(seeds[5], (RANK, SUBTREES * LOCAL_NODES * RANK), RANK ** -0.5, 0.75, ((1, 32),), jnp.float32),
        "far_partner": draw_far_partner(jax.random.fold_in(seeds[11], 71), 0),
        "dev_transfer": draw_dev_transfer(jax.random.fold_in(seeds[11], 71), 0),
        "dev_coupling": gaussian(seeds[8], (GROUPS, RANK, DEV_NODES * RANK), (2.0 / RANK ** 0.5), 4.0, ((0, 4),), jnp.float32),
        "grp_transfer": draw_grp_transfer(jax.random.fold_in(seeds[11], 71), 0),
        "grp_coupling": gaussian(seeds[10], (RANK, GRP_NODES * RANK), (6.0 / RANK ** 0.5), 6.0, (), jnp.float32),
    }


precise = lax.Precision.HIGHEST

def blocks_of(matrix, node_count):
    return matrix.reshape(matrix.shape[0], node_count, -1).transpose(1, 0, 2)

def lower_solve(factor, right_side, transpose):
    return jax.scipy.linalg.solve_triangular(factor, right_side, trans=transpose, lower=True)

def combine(factors, projected, transfers):
    upper_blocks = jnp.einsum('nji,njk->nik', factors, transfers, precision=precise)
    even_upper = upper_blocks[0::2]
    odd_upper = upper_blocks[1::2]
    gram_matrix = jnp.einsum('nji,njk->nik', even_upper, even_upper, precision=precise) + jnp.einsum('nji,njk->nik', odd_upper, odd_upper, precision=precise)
    parent = jnp.linalg.cholesky(gram_matrix)
    summed = jnp.einsum('nji,njr->nir', even_upper, projected[0::2], precision=precise) + jnp.einsum('nji,njr->nir', odd_upper, projected[1::2], precision=precise)
    return (upper_blocks, parent, lower_solve(parent, summed, 0))

def sibling(stacked):
    return stacked.reshape((-1, 2) + stacked.shape[1:])[:, ::-1].reshape(stacked.shape)

def reference(rhs, leaf_basis, near_blocks, near_partner, local_transfer, local_coupling, far_partner, dev_transfer, dev_coupling, grp_transfer, grp_coupling):
    leaf_bases = leaf_basis.reshape(LEAF, LEAVES, RANK).transpose(1, 0, 2)
    points = rhs.reshape(NRHS, LEAVES, LEAF)
    factors = jnp.linalg.cholesky(jnp.einsum('lpi,lpk->lik', leaf_bases, leaf_bases, precision=precise))
    projected = lower_solve(factors, jnp.einsum('lpk,rlp->lkr', leaf_bases, points, precision=precise), 0)
    local_trans = local_transfer.reshape(RANK, SUBTREES, LOCAL_NODES, RANK).transpose(1, 2, 0, 3)
    local_couple = local_coupling.reshape(RANK, SUBTREES, LOCAL_NODES, RANK).transpose(1, 2, 0, 3)
    dev_trans = dev_transfer.reshape(GROUPS, RANK, DEV_NODES, RANK).transpose(0, 2, 1, 3)
    dev_couple = dev_coupling.reshape(GROUPS, RANK, DEV_NODES, RANK).transpose(0, 2, 1, 3)
    grp_trans = blocks_of(grp_transfer, GRP_NODES)
    grp_couple = blocks_of(grp_coupling, GRP_NODES)
    level_factors = [factors]
    level_upper = []
    level_coupled = []
    offset = 0
    for tree_level in range(LOC):
        level_nodes = LEAF_DEV >> tree_level
        transfers = local_trans[:, offset:offset + level_nodes].reshape(-1, RANK, RANK)
        couplings = local_couple[:, offset:offset + level_nodes].reshape(-1, RANK, RANK)
        partners = far_partner[:, offset:offset + level_nodes].reshape(-1)
        level_coupled.append(jnp.einsum('nik,nkr->nir', couplings, projected[partners], precision=precise))
        upper_blocks, factors, projected = combine(factors, projected, transfers)
        level_upper.append(upper_blocks)
        level_factors.append(factors)
        offset += level_nodes
    offset = 0
    for tree_level in range(LOG_DEV):
        level_nodes = N_DEV >> tree_level
        transfers = dev_trans[:, offset:offset + level_nodes].reshape(-1, RANK, RANK)
        couplings = dev_couple[:, offset:offset + level_nodes].reshape(-1, RANK, RANK)
        level_coupled.append(jnp.einsum('nik,nkr->nir', couplings, sibling(projected), precision=precise))
        upper_blocks, factors, projected = combine(factors, projected, transfers)
        level_upper.append(upper_blocks)
        level_factors.append(factors)
        offset += level_nodes
    offset = 0
    for tree_level in range(LOG_GRP):
        level_nodes = N_GRP >> tree_level
        transfers = grp_trans[offset:offset + level_nodes]
        couplings = grp_couple[offset:offset + level_nodes]
        level_coupled.append(jnp.einsum('nik,nkr->nir', couplings, sibling(projected), precision=precise))
        upper_blocks, factors, projected = combine(factors, projected, transfers)
        level_upper.append(upper_blocks)
        level_factors.append(factors)
        offset += level_nodes
    root_factor = factors[0]
    downward = jnp.zeros((1, RANK, NRHS), jnp.float32)
    for tree_level in reversed(range(len(level_upper))):
        lifted = lower_solve(level_factors[tree_level + 1], downward, 1)
        downward = level_coupled[tree_level] + jnp.einsum('nik,nkr->nir', level_upper[tree_level], jnp.repeat(lifted, 2, axis=0), precision=precise)
    lifted = lower_solve(level_factors[0], downward, 1)
    far_part = jnp.einsum('lpk,lkr->rlp', leaf_bases, lifted, precision=precise)
    near_grid = near_blocks.reshape(LEAF, LEAVES, 2, LEAF)
    near_part = jnp.einsum('plq,rlq->rlp', near_grid[:, :, 0], points, precision=precise) + jnp.einsum('plq,rlq->rlp', near_grid[:, :, 1], points[:, near_partner], precision=precise)
    product = (near_part + far_part).reshape(NRHS, UNKNOWNS)
    return (product, root_factor)
```

```python
import functools

import jax
import jax.numpy as jnp
from jax import lax
from jax.experimental import pallas as pl
from jax.experimental.pallas import tpu as pltpu
from jax.sharding import PartitionSpec as P

RANK = 64
LEAF = 64
NRHS = 16
LOC = 4
LEAF_DEV = 16
LOCAL_NODES = 30
PAIR = 2 * RANK
LANES = 128
BATCH = 32
ROWS = RANK + NRHS
PAIRS = LOCAL_NODES // 2
POINT_SPAN = LEAF_DEV * LEAF
NODE_SPAN = LOCAL_NODES * RANK
OFFSETS = [2 * LEAF_DEV - 2 * (LEAF_DEV >> level) for level in range(LOC)]
MIB = 1 << 20

precise = lax.Precision.HIGHEST


def mm(a, b):
    return lax.dot_general(
        a, b, (((1,), (0,)), ((), ())), precision=precise, preferred_element_type=jnp.float32
    )


def mm_t(a, b):
    return lax.dot_general(
        a, b, (((1,), (1,)), ((), ())), precision=precise, preferred_element_type=jnp.float32
    )


def low_half(rows):
    return lax.broadcasted_iota(jnp.int32, (rows, PAIR), 1) < RANK


def swap_halves(x):
    return pltpu.roll(x, RANK, 1)


def spread_pair(pair):
    low = low_half(pair.shape[0])
    return jnp.concatenate([jnp.where(low, pair, 0.0), jnp.where(low, 0.0, pair)], axis=0)


def stack_low(pair):
    low = low_half(pair.shape[0])
    return jnp.concatenate(
        [jnp.where(low, pair, 0.0), jnp.where(low, swap_halves(pair), 0.0)], axis=0
    )


def stack_high(pair):
    low = low_half(pair.shape[0])
    return jnp.concatenate(
        [jnp.where(low, 0.0, swap_halves(pair)), jnp.where(low, 0.0, pair)], axis=0
    )


def factor_batch(a, m):
    blocks = RANK // 8
    sub = lax.broadcasted_iota(jnp.int32, (8, LANES), 0)
    for kb in range(blocks):
        k0 = 8 * kb
        rows = [a[k0 + k, k0:RANK, :] for k in range(8)]
        mrows = []
        for k in range(8):
            unit = (sub == k).astype(jnp.float32)
            mrows.append(jnp.concatenate([m[k0 + k, 0:k0, :], unit], axis=0) if kb else unit)
        for k in range(8):
            scale = lax.rsqrt(rows[k][k : k + 1, :])
            rows[k] = rows[k] * scale
            mrows[k] = mrows[k] * scale
            for k2 in range(k + 1, 8):
                f = rows[k][k2 : k2 + 1, :]
                rows[k2] = rows[k2] - f * rows[k]
                mrows[k2] = mrows[k2] - f * mrows[k]
        for k in range(8):
            a[k0 + k, k0:RANK, :] = rows[k]
            m[k0 + k, 0 : k0 + 8, :] = mrows[k]
            if kb + 1 < blocks:
                m[k0 + k, k0 + 8 : RANK, :] = jnp.zeros((RANK - k0 - 8, LANES), jnp.float32)
        for ib in range(kb + 1, blocks):
            for i in range(8 * ib, 8 * ib + 8):
                acc = a[i, 8 * ib : RANK, :]
                old = m[i, 0:k0, :] if kb else None
                new = None
                for k in range(8):
                    f = a[k0 + k, i : i + 1, :]
                    acc = acc - f * a[k0 + k, 8 * ib : RANK, :]
                    part = f * m[k0 + k, 0 : k0 + 8, :]
                    if kb:
                        old = old - part[0:k0]
                    tail = part[k0 : k0 + 8]
                    new = -tail if new is None else new - tail
                a[i, 8 * ib : RANK, :] = acc
                if kb:
                    m[i, 0:k0, :] = old
                m[i, k0 : k0 + 8, :] = new


def invert_nodes(d, a, m, inv, count):
    for i in range(RANK):
        rows = d[pl.ds(i, count, stride=RANK), :]
        a[i, :, 0:count] = rows.T[0:RANK]
    factor_batch(a, m)
    for i in range(RANK):
        inv[pl.ds(i, count, stride=RANK), :] = m[i, :, 0:count].T


def gram_kernel(basis, rhs, transfer, gram, z_out, top):
    blocks = []
    zs = []
    for p in range(LEAF_DEV // 2):
        lanes = slice(PAIR * p, PAIR * (p + 1))
        u = basis[:, lanes]
        spread = spread_pair(u)
        full = mm(u.T, u)
        low = low_half(RANK)
        blocks.append(
            jnp.concatenate(
                [jnp.where(low, full[:RANK], 0.0), jnp.where(low, 0.0, full[RANK:])], axis=0
            )
        )
        zs.append(mm(rhs[:, lanes], spread))
    tile = 0
    for level in range(LOC):
        pairs = len(blocks)
        for p in range(pairs):
            gram[tile + p] = blocks[p]
            z_out[:, PAIR * (tile + p) : PAIR * (tile + p + 1)] = zs[p]
        next_blocks = []
        next_zs = []
        for q in range((pairs + 1) // 2):
            first = transfer[:, PAIR * (tile + 2 * q) : PAIR * (tile + 2 * q + 1)]
            f = stack_low(first)
            h = mm(blocks[2 * q], f)
            z = mm(zs[2 * q], f)
            parent = mm(f.T, h)
            if pairs > 1:
                second = transfer[:, PAIR * (tile + 2 * q + 1) : PAIR * (tile + 2 * q + 2)]
                f = stack_high(second)
                h = mm(blocks[2 * q + 1], f)
                z = z + mm(zs[2 * q + 1], f)
                parent = parent + mm(f.T, h)
            next_blocks.append(parent)
            next_zs.append(z)
        tile += pairs
        blocks = next_blocks
        zs = next_zs
    top[0:RANK, :] = blocks[0][0:RANK, 0:RANK]
    top[RANK:ROWS, :] = zs[0][:, 0:RANK]


def local_kernel(gram, z, rhs, inv, packed, d, a, m):
    for p in range(PAIRS):
        d[PAIR * p : PAIR * p + RANK, :] = gram[p, 0:RANK, :]
        d[PAIR * p + RANK : PAIR * (p + 1), :] = swap_halves(gram[p, RANK:PAIR, :])
    invert_nodes(d, a, m, inv, BATCH)
    packed[:, 0:POINT_SPAN] = rhs[...]
    for p in range(PAIRS):
        pair = z[:, PAIR * p : PAIR * (p + 1)]
        even = mm_t(pair[:, 0:RANK], inv[PAIR * p : PAIR * p + RANK, :])
        odd = mm_t(pair[:, RANK:PAIR], inv[PAIR * p + RANK : PAIR * (p + 1), :])
        packed[:, POINT_SPAN + PAIR * p : POINT_SPAN + PAIR * (p + 1)] = jnp.concatenate(
            [even, odd], axis=1
        )


def merge(nodes, tile, transfer):
    parents = []
    for p in range(len(nodes) // 2):
        pair = transfer[:, pl.ds(pl.multiple_of(PAIR * (tile + p), PAIR), PAIR)]
        even, odd = pair[:, 0:RANK], pair[:, RANK:PAIR]
        he, ho = mm(nodes[2 * p], even), mm(nodes[2 * p + 1], odd)
        g = mm(even.T, he[0:RANK]) + mm(odd.T, ho[0:RANK])
        parents.append(jnp.concatenate([g, he[RANK:] + ho[RANK:]], axis=0))
    return parents


def climb(blocks, place, start, bits, count, transfer, stack, records, first_record):
    for k, block in enumerate(blocks):
        stack[k] = block[...]
    here = lax.shift_right_logical(place, start)
    low = here & (2**bits - 1)
    base = here - low
    nodes = [stack[c ^ low] for c in range(2**bits)]
    for level in range(start, start + bits):
        m = count >> level
        own, sibling = (0, 1) if level == start else (low, low ^ 1)
        records[2 * (first_record + level - start)] = stack[own]
        records[2 * (first_record + level - start) + 1] = stack[sibling]
        tile = (2 * count - 2 * m + base) // 2
        nodes = merge(nodes, tile, transfer)
        low = lax.shift_right_logical(low, 1)
        base = lax.shift_right_logical(base, 1)
        for c, node in enumerate(nodes):
            stack[c] = node
    return nodes[0]


def climb_kernel(start, bits, count, place, transfer, *refs):
    blocks = refs[: 2**bits]
    top, records, stack = refs[2**bits :]
    top[...] = climb(blocks, place[0], start, bits, count, transfer, stack, records, 0)


def couple_kernel(
    place,
    near_partner,
    far_partner,
    own,
    lower,
    upper,
    inv,
    coupling,
    transfer,
    basis,
    near,
    base,
    lift,
    window,
):
    packed_tiles = (POINT_SPAN + NODE_SPAN) // PAIR
    point_tiles = POINT_SPAN // PAIR
    starts = [point_tiles + OFFSETS[level] // 2 for level in range(LOC)]
    spans = [(0, point_tiles)] + [(starts[level], (LEAF_DEV >> level) // 2) for level in range(LOC)]
    firsts = []
    slot = 0
    for start, span in spans:
        firsts.append(slot)
        for source in (lower, own, upper):
            for t in range(span):
                tile = source[:, PAIR * (start + t) : PAIR * (start + t + 1)]
                window[0, slot] = tile
                window[1, slot] = swap_halves(tile)
                slot += 1

    def pick(first, index, parity):
        return window[(index & 1) ^ parity, first + lax.shift_right_logical(index, 1)]

    low16 = low_half(NRHS)
    lifted = []
    for level in range(LOC):
        m = LEAF_DEV >> level
        tiles = []
        for p in range(m // 2):
            node = OFFSETS[level] + 2 * p
            sides = []
            for side in range(2):
                index = far_partner[0, node + side] - (place[0] - 1) * m
                value = pick(firsts[level + 1], index, 0)[:, 0:RANK]
                s = coupling[:, PAIR * (node // 2) : PAIR * (node // 2 + 1)]
                y = mm_t(value, s[:, RANK * side : RANK * (side + 1)])
                rows = slice(RANK * (node + side), RANK * (node + side + 1))
                sides.append(mm(y, inv[rows, :]))
            tiles.append(jnp.concatenate(sides, axis=1))
        lifted.append(tiles)

    state = None
    for level in reversed(range(LOC)):
        m = LEAF_DEV >> level
        tile = OFFSETS[level] // 2
        next_state = []
        for p in range(m // 2):
            pair = transfer[:, PAIR * (tile + p) : PAIR * (tile + p + 1)]
            if state is None:
                f = stack_low(pair)
                rows = f[:, 0:RANK].T
                next_state.append(jnp.concatenate([lifted[level][p], rows], axis=0))
                continue
            f = stack_high(pair) if p % 2 else stack_low(pair)
            rows = mm_t(state[p // 2], f)
            next_state.append(
                jnp.concatenate([rows[0:NRHS] + lifted[level][p], rows[NRHS:]], axis=0)
            )
        state = next_state

    for p in range(LEAF_DEV // 2):
        lanes = slice(PAIR * p, PAIR * (p + 1))
        out = mm_t(state[p], spread_pair(basis[:, lanes]))
        own_points = own[:, lanes]
        swapped = swap_halves(own_points)
        inputs = []
        for side in range(2):
            index = near_partner[2 * p + side] - (place[0] - 1) * LEAF_DEV
            value = pick(0, index, 1)
            inputs.append(jnp.where(low16, swapped if side else own_points, value))
        weights = jnp.concatenate(
            [
                near[:, 2 * PAIR * p : 2 * PAIR * p + PAIR],
                near[:, 2 * PAIR * p + PAIR : 2 * PAIR * (p + 1)],
            ],
            axis=0,
        )
        near_out = mm_t(jnp.concatenate(inputs, axis=0), weights)
        base[:, lanes] = out[0:NRHS] + jnp.where(low16, near_out[0:NRHS], near_out[NRHS:])
        lift[:, lanes] = out[NRHS:]


def half_of(array, index):
    pair = array[:, pl.ds(pl.multiple_of(PAIR * (index // 2), PAIR), PAIR)]
    return jnp.where(index % 2 == 1, pair[:, RANK:], pair[:, 0:RANK])


def top_kernel(
    grp_count,
    dev_count,
    start,
    bits,
    record_spans,
    place,
    grp_transfer,
    grp_coupling,
    dev_transfer,
    dev_coupling,
    base,
    lift,
    *refs,
):
    blocks = refs[: 2**bits]
    refs = refs[2**bits :]
    earlier = refs[: len(record_spans)]
    product, root, stack, records, d, a, m, inv = refs[len(record_spans) :]
    level = 0
    for ref, span in zip(earlier, record_spans):
        for r in range(2 * span):
            records[2 * level + r] = ref[r]
        level += span
    top = climb(
        blocks, place[0], start, bits, grp_count, grp_transfer, stack, records, level
    )
    levels = level + bits
    batch = inv.shape[0] // RANK
    for r in range(2 * levels):
        d[RANK * r : RANK * (r + 1), 0:RANK] = records[r, 0:RANK]
    d[RANK * 2 * levels : RANK * (2 * levels + 1), 0:RANK] = top[0:RANK]
    invert_nodes(d, a, m, inv, batch)
    root_inverse = inv[RANK * 2 * levels : RANK * (2 * levels + 1), :]
    keep = lax.broadcasted_iota(jnp.int32, (RANK, RANK), 0) >= lax.broadcasted_iota(
        jnp.int32, (RANK, RANK), 1
    )
    root[...] = jnp.where(keep, mm_t(top[0:RANK], root_inverse), 0.0)
    dev_levels = dev_count.bit_length() - 1
    terms = []
    for n in range(levels):
        if n < dev_levels:
            count, shift, spot = dev_count, n, place[1]
            transfer, coupling = dev_transfer, dev_coupling
        else:
            count, shift, spot = grp_count, n - dev_levels, place[0]
            transfer, coupling = grp_transfer, grp_coupling
        index = 2 * count - 2 * (count >> shift) + lax.shift_right_logical(spot, shift)
        other = records[2 * n + 1, RANK:ROWS]
        xhat = mm_t(other, inv[RANK * (2 * n + 1) : RANK * (2 * n + 2), :])
        yhat = mm_t(xhat, half_of(coupling, index))
        terms.append((mm(yhat, inv[RANK * 2 * n : RANK * (2 * n + 1), :]), half_of(transfer, index)))
    value = None
    for term, transfer in reversed(terms):
        value = term if value is None else term + mm_t(value, transfer)
    product[...] = base[...] + mm(value, lift[...])


def vmem(count):
    return [pl.BlockSpec(memory_space=pltpu.VMEM)] * count


def smem(count):
    return [pl.BlockSpec(memory_space=pltpu.SMEM)] * count


def f32(*shape):
    return jax.ShapeDtypeStruct(shape, jnp.float32)


def params(mib):
    return pltpu.CompilerParams(vmem_limit_bytes=mib * MIB)


def cost(flops, size):
    return pl.CostEstimate(flops=flops, bytes_accessed=size, transcendentals=0)


def exchange(block, axis, start, bits):
    count = lax.axis_size(axis)
    return [block] + [
        lax.ppermute(block, axis, [(i, i ^ (k << start)) for i in range(count)])
        for k in range(1, 2**bits)
    ]


def chunks(levels, first):
    out = []
    start = 0
    while start < levels:
        bits = min(first if start == 0 else 2, levels - start)
        out.append((start, bits))
        start += bits
    return out


def climb_call(blocks, place, start, bits, count, transfer):
    return pl.pallas_call(
        functools.partial(climb_kernel, start, bits, count),
        out_shape=[f32(ROWS, RANK), f32(2 * bits, ROWS, RANK)],
        in_specs=smem(1) + vmem(1 + 2**bits),
        out_specs=vmem(2),
        scratch_shapes=[pltpu.VMEM((2**bits, ROWS, RANK), jnp.float32)],
        compiler_params=params(8),
        name="climb",
    )(place, transfer, *blocks)


def shards(
    rhs,
    leaf_basis,
    near_blocks,
    near_partner,
    local_transfer,
    local_coupling,
    far_partner,
    dev_transfer,
    dev_coupling,
    grp_transfer,
    grp_coupling,
):
    dev_count = lax.axis_size("dev")
    grp_count = lax.axis_size("grp")
    dev_place = lax.axis_index("dev").astype(jnp.int32)
    grp_place = lax.axis_index("grp").astype(jnp.int32)
    places = jnp.stack([grp_place, dev_place])
    dev_spot = dev_place[None]
    device_spot = (grp_place * dev_count + dev_place)[None]

    gram, z, top = pl.pallas_call(
        gram_kernel,
        out_shape=[f32(PAIRS, PAIR, PAIR), f32(NRHS, NODE_SPAN), f32(ROWS, RANK)],
        in_specs=vmem(3),
        out_specs=vmem(3),
        compiler_params=params(16),
        name="gram",
    )(leaf_basis, rhs, local_transfer)

    records = []
    spans = []
    dev_transfer = dev_transfer[0]
    dev_coupling = dev_coupling[0]
    for start, bits in chunks(dev_count.bit_length() - 1, 1):
        blocks = exchange(top, "dev", start, bits)
        top, record = climb_call(blocks, dev_spot, start, bits, dev_count, dev_transfer)
        records.append(record)
        spans.append(bits)

    inv, packed = pl.pallas_call(
        local_kernel,
        out_shape=[f32(BATCH * RANK, RANK), f32(NRHS, POINT_SPAN + NODE_SPAN)],
        in_specs=vmem(3),
        out_specs=vmem(2),
        scratch_shapes=[
            pltpu.VMEM((BATCH * RANK, LANES), jnp.float32),
            pltpu.VMEM((RANK, RANK, LANES), jnp.float32),
            pltpu.VMEM((RANK, RANK, LANES), jnp.float32),
        ],
        compiler_params=params(24),
        name="local_factors",
    )(gram, z, rhs)

    both = ("grp", "dev")
    ends = grp_count * dev_count - 1
    lower = lax.ppermute(packed, both, [(i, i + 1) for i in range(ends)])
    upper = lax.ppermute(packed, both, [(i + 1, i) for i in range(ends)])

    window_tiles = 3 * (POINT_SPAN + NODE_SPAN) // PAIR
    base, lift = pl.pallas_call(
        couple_kernel,
        out_shape=[f32(NRHS, POINT_SPAN), f32(RANK, POINT_SPAN)],
        in_specs=smem(3) + vmem(8),
        out_specs=vmem(2),
        scratch_shapes=[pltpu.VMEM((2, window_tiles, NRHS, PAIR), jnp.float32)],
        compiler_params=params(24),
        name="couple",
    )(
        device_spot,
        near_partner,
        far_partner,
        packed,
        lower,
        upper,
        inv,
        local_coupling,
        local_transfer,
        leaf_basis,
        near_blocks,
    )

    grp_chunks = chunks(grp_count.bit_length() - 1, 2)
    for start, bits in grp_chunks[:-1]:
        blocks = exchange(top, "grp", start, bits)
        top, record = climb_call(blocks, grp_place[None], start, bits, grp_count, grp_transfer)
        records.append(record)
        spans.append(bits)
    start, bits = grp_chunks[-1]
    blocks = exchange(top, "grp", start, bits)
    levels = sum(spans) + bits
    batch = 8 * ((2 * levels + 1 + 7) // 8)
    return pl.pallas_call(
        functools.partial(top_kernel, grp_count, dev_count, start, bits, tuple(spans)),
        out_shape=[f32(NRHS, POINT_SPAN), f32(RANK, RANK)],
        in_specs=smem(1) + vmem(6 + len(blocks) + len(records)),
        out_specs=vmem(2),
        scratch_shapes=[
            pltpu.VMEM((2**bits, ROWS, RANK), jnp.float32),
            pltpu.VMEM((2 * levels, ROWS, RANK), jnp.float32),
            pltpu.VMEM((batch * RANK, LANES), jnp.float32),
            pltpu.VMEM((RANK, RANK, LANES), jnp.float32),
            pltpu.VMEM((RANK, RANK, LANES), jnp.float32),
            pltpu.VMEM((batch * RANK, RANK), jnp.float32),
        ],
        compiler_params=params(24),
        name="top",
    )(
        places,
        grp_transfer,
        grp_coupling,
        dev_transfer,
        dev_coupling,
        base,
        lift,
        *blocks,
        *records,
    )


def solution(mesh):
    return jax.shard_map(
        shards,
        mesh=mesh,
        in_specs=(
            P(None, ("grp", "dev")),
            P(None, ("grp", "dev")),
            P(None, ("grp", "dev")),
            P(("grp", "dev")),
            P(None, ("grp", "dev")),
            P(None, ("grp", "dev")),
            P(("grp", "dev"), None),
            P("grp", None, None),
            P("grp", None, None),
            P(),
            P(),
        ),
        out_specs=(P(None, ("grp", "dev")), P()),
        check_vma=False,
    )
```

```python
import functools

import jax
import jax.numpy as jnp
from jax import lax
from jax.experimental import pallas as pl
from jax.experimental.pallas import tpu as pltpu
from jax.sharding import PartitionSpec as P

RANK = 64
LEAF = 64
NRHS = 16
LOC = 4
LEAF_DEV = 16
LOCAL_NODES = 30
PAIR = 2 * RANK
LANES = 128
BATCH = 16
ROWS = RANK + NRHS
PAIRS = LOCAL_NODES // 2
POINT_SPAN = LEAF_DEV * LEAF
NODE_SPAN = LOCAL_NODES * RANK
OFFSETS = [2 * LEAF_DEV - 2 * (LEAF_DEV >> level) for level in range(LOC)]
MIB = 1 << 20

precise = lax.Precision.HIGHEST


def halves(x):
    high = x.astype(jnp.bfloat16)
    return high, (x - high.astype(jnp.float32)).astype(jnp.bfloat16)


def three_pass(a, b, side):
    dims = (((1,), (side,)), ((), ()))
    dot = functools.partial(
        lax.dot_general, dimension_numbers=dims, preferred_element_type=jnp.float32
    )
    a_high, a_low = halves(a)
    b_high, b_low = halves(b)
    return dot(a_high, b_high) + (dot(a_high, b_low) + dot(a_low, b_high))


def full(a, b, side):
    dims = (((1,), (side,)), ((), ()))
    return lax.dot_general(a, b, dims, precision=precise, preferred_element_type=jnp.float32)


def mm(a, b):
    return three_pass(a, b, 0)


def mm_t(a, b):
    return three_pass(a, b, 1)


def mm_full(a, b):
    return full(a, b, 0)


def low_half(rows):
    return lax.broadcasted_iota(jnp.int32, (rows, PAIR), 1) < RANK


def swap_halves(x):
    return pltpu.roll(x, RANK, 1)


def spread_pair(pair):
    low = low_half(pair.shape[0])
    return jnp.concatenate([jnp.where(low, pair, 0.0), jnp.where(low, 0.0, pair)], axis=0)


def stack_low(pair):
    low = low_half(pair.shape[0])
    return jnp.concatenate(
        [jnp.where(low, pair, 0.0), jnp.where(low, swap_halves(pair), 0.0)], axis=0
    )


def stack_high(pair):
    low = low_half(pair.shape[0])
    return jnp.concatenate(
        [jnp.where(low, 0.0, swap_halves(pair)), jnp.where(low, 0.0, pair)], axis=0
    )


def factor_batch(a, m):
    blocks = RANK // 8
    sub = lax.broadcasted_iota(jnp.int32, (8, LANES), 0)
    for kb in range(blocks):
        k0 = 8 * kb
        rows = [a[k0 + k, k0:RANK, :] for k in range(8)]
        mrows = []
        for k in range(8):
            unit = (sub == k).astype(jnp.float32)
            mrows.append(jnp.concatenate([m[k0 + k, 0:k0, :], unit], axis=0) if kb else unit)
        for k in range(8):
            scale = lax.rsqrt(rows[k][k : k + 1, :])
            rows[k] = rows[k] * scale
            mrows[k] = mrows[k] * scale
            for k2 in range(k + 1, 8):
                f = rows[k][k2 : k2 + 1, :]
                rows[k2] = rows[k2] - f * rows[k]
                mrows[k2] = mrows[k2] - f * mrows[k]
        for k in range(8):
            a[k0 + k, k0:RANK, :] = rows[k]
            m[k0 + k, 0 : k0 + 8, :] = mrows[k]
            if kb + 1 < blocks:
                m[k0 + k, k0 + 8 : RANK, :] = jnp.zeros((RANK - k0 - 8, LANES), jnp.float32)
        for ib in range(kb + 1, blocks):
            for i in range(8 * ib, 8 * ib + 8):
                acc = a[i, 8 * ib : RANK, :]
                old = m[i, 0:k0, :] if kb else None
                new = None
                for k in range(8):
                    f = a[k0 + k, i : i + 1, :]
                    acc = acc - f * a[k0 + k, 8 * ib : RANK, :]
                    part = f * m[k0 + k, 0 : k0 + 8, :]
                    if kb:
                        old = old - part[0:k0]
                    tail = part[k0 : k0 + 8]
                    new = -tail if new is None else new - tail
                a[i, 8 * ib : RANK, :] = acc
                if kb:
                    m[i, 0:k0, :] = old
                m[i, k0 : k0 + 8, :] = new


def invert_pairs(gram, a, m, inv, count):
    for i in range(RANK):
        rows = gram[pl.ds(i, count, stride=RANK), :]
        both = jnp.concatenate([rows, swap_halves(rows)], axis=0)
        a[i, :, 0 : 2 * count] = both[:, 0:RANK].T
    factor_batch(a, m)
    for i in range(RANK):
        rows = m[i, :, 0 : 2 * count].T
        inv[pl.ds(i, count, stride=RANK), :] = jnp.concatenate([rows[:count], rows[count:]], axis=1)


def gram_kernel(basis_in, rhs_in, transfer_in, gram, z_out, top, basis, rhs, transfer, sems):
    copies = [
        pltpu.make_async_copy(source, target, sems.at[n])
        for n, (source, target) in enumerate(
            ((basis_in, basis), (rhs_in, rhs), (transfer_in, transfer))
        )
    ]
    for copy in copies:
        copy.start()
    copies[0].wait()
    copies[1].wait()
    blocks = []
    zs = []
    for p in range(LEAF_DEV // 2):
        lanes = slice(PAIR * p, PAIR * (p + 1))
        u = basis[:, lanes]
        spread = spread_pair(u)
        full = mm(u.T, u)
        low = low_half(RANK)
        blocks.append(
            jnp.concatenate(
                [jnp.where(low, full[:RANK], 0.0), jnp.where(low, 0.0, full[RANK:])], axis=0
            )
        )
        zs.append(mm(rhs[:, lanes], spread))
    copies[2].wait()
    tile = 0
    for level in range(LOC):
        pairs = len(blocks)
        for p in range(pairs):
            gram[RANK * (tile + p) : RANK * (tile + p + 1), :] = jnp.where(
                low_half(RANK), blocks[p][:RANK], blocks[p][RANK:]
            )
            z_out[:, PAIR * (tile + p) : PAIR * (tile + p + 1)] = zs[p]
        next_blocks = []
        next_zs = []
        for q in range((pairs + 1) // 2):
            first = transfer[:, PAIR * (tile + 2 * q) : PAIR * (tile + 2 * q + 1)]
            f = stack_low(first)
            h = mm(blocks[2 * q], f)
            z = mm(zs[2 * q], f)
            parent = mm(f.T, h)
            if pairs > 1:
                second = transfer[:, PAIR * (tile + 2 * q + 1) : PAIR * (tile + 2 * q + 2)]
                f = stack_high(second)
                h = mm(blocks[2 * q + 1], f)
                z = z + mm(zs[2 * q + 1], f)
                parent = parent + mm(f.T, h)
            next_blocks.append(parent)
            next_zs.append(z)
        tile += pairs
        blocks = next_blocks
        zs = next_zs
    top[0:RANK, :] = blocks[0][0:RANK, 0:RANK]
    top[RANK:ROWS, :] = zs[0][:, 0:RANK]


def pair_rows(p):
    return slice(RANK * p, RANK * (p + 1))


def pair_lanes(p):
    return slice(PAIR * p, PAIR * (p + 1))


def local_kernel(gram, z, rhs, after, inv, packed, a, m):
    invert_pairs(gram, a, m, inv, BATCH)
    packed[:, 0:POINT_SPAN] = rhs[...]
    for p in range(PAIRS):
        packed[:, POINT_SPAN + PAIR * p : POINT_SPAN + PAIR * (p + 1)] = mm_t(
            z[:, pair_lanes(p)], spread_pair(inv[pair_rows(p), :])
        )


def merge(nodes, tile, transfer):
    parents = []
    for p in range(len(nodes) // 2):
        pair = transfer[:, pl.ds(pl.multiple_of(PAIR * (tile + p), PAIR), PAIR)]
        even, odd = pair[:, 0:RANK], pair[:, RANK:PAIR]
        he, ho = mm(nodes[2 * p], even), mm(nodes[2 * p + 1], odd)
        g = mm(even.T, he[0:RANK]) + mm(odd.T, ho[0:RANK])
        parents.append(jnp.concatenate([g, he[RANK:] + ho[RANK:]], axis=0))
    return parents


def climb(blocks, place, start, bits, count, transfer, stack, records, first_record):
    for k, block in enumerate(blocks):
        stack[k] = block[...]
    here = lax.shift_right_logical(place, start)
    low = here & (2**bits - 1)
    base = here - low
    nodes = [stack[c ^ low] for c in range(2**bits)]
    for level in range(start, start + bits):
        m = count >> level
        own, sibling = (0, 1) if level == start else (low, low ^ 1)
        records[2 * (first_record + level - start)] = stack[own]
        records[2 * (first_record + level - start) + 1] = stack[sibling]
        tile = (2 * count - 2 * m + base) // 2
        nodes = merge(nodes, tile, transfer)
        low = lax.shift_right_logical(low, 1)
        base = lax.shift_right_logical(base, 1)
        for c, node in enumerate(nodes):
            stack[c] = node
    return nodes[0]


def climb_kernel(axis, start, bits, count, transfer, *refs):
    blocks = refs[: 2**bits]
    top, records = refs[-3 - (len(refs) - 2**bits - 3) // 2 :][:2]
    stack = refs[-1]
    top[...] = climb(blocks, lax.axis_index(axis), start, bits, count, transfer, stack, records, 0)


def couple_kernel(
    near_partner_in,
    far_partner_in,
    own,
    twin,
    beside,
    inv,
    coupling,
    transfer,
    basis,
    near,
    base,
    lift,
    window,
    near_partner,
    far_partner,
    sems,
):
    copies = [
        pltpu.make_async_copy(near_partner_in, near_partner, sems.at[0]),
        pltpu.make_async_copy(far_partner_in, far_partner, sems.at[1]),
    ]
    for copy in copies:
        copy.start()
    packed_tiles = (POINT_SPAN + NODE_SPAN) // PAIR
    point_tiles = POINT_SPAN // PAIR
    starts = [point_tiles + OFFSETS[level] // 2 for level in range(LOC)]
    spans = [(0, point_tiles)] + [(starts[level], (LEAF_DEV >> level) // 2) for level in range(LOC)]
    firsts = []
    slot = 0
    place = lax.axis_index("grp") * lax.axis_size("dev") + lax.axis_index("dev")
    odd = place & 1
    for start, span in spans:
        firsts.append(slot)
        for source, shift in ((beside, odd), (own, None), (twin, 1 - odd)):
            first = slot + span if shift is None else slot + 2 * span * shift
            for t in range(span):
                tile = source[:, PAIR * (start + t) : PAIR * (start + t + 1)]
                window[0, first + t] = tile
                window[1, first + t] = swap_halves(tile)
        slot += 3 * span

    for copy in copies:
        copy.wait()

    def pick(first, index, parity):
        return window[(index & 1) ^ parity, first + lax.shift_right_logical(index, 1)]

    low16 = low_half(NRHS)
    lifted = []
    for level in range(LOC):
        m = LEAF_DEV >> level
        tiles = []
        for p in range(m // 2):
            node = OFFSETS[level] + 2 * p
            values = []
            for side in range(2):
                index = far_partner[0, node + side] - (place - 1) * m
                values.append(pick(firsts[level + 1], index, side))
            xhat = jnp.where(low16, values[0], values[1])
            y = mm_t(xhat, spread_pair(coupling[:, pair_lanes(node // 2)]))
            tiles.append(mm(y, spread_pair(inv[pair_rows(node // 2), :])))
        lifted.append(tiles)

    state = None
    for level in reversed(range(LOC)):
        m = LEAF_DEV >> level
        tile = OFFSETS[level] // 2
        next_state = []
        for p in range(m // 2):
            pair = transfer[:, PAIR * (tile + p) : PAIR * (tile + p + 1)]
            if state is None:
                f = stack_low(pair)
                rows = f[:, 0:RANK].T
                next_state.append(jnp.concatenate([lifted[level][p], rows], axis=0))
                continue
            f = stack_high(pair) if p % 2 else stack_low(pair)
            rows = mm_t(state[p // 2], f)
            next_state.append(
                jnp.concatenate([rows[0:NRHS] + lifted[level][p], rows[NRHS:]], axis=0)
            )
        state = next_state

    for p in range(LEAF_DEV // 2):
        lanes = slice(PAIR * p, PAIR * (p + 1))
        out = mm_t(state[p], spread_pair(basis[:, lanes]))
        own_points = own[:, lanes]
        swapped = swap_halves(own_points)
        inputs = []
        for side in range(2):
            index = near_partner[2 * p + side] - (place - 1) * LEAF_DEV
            value = pick(0, index, 1)
            inputs.append(jnp.where(low16, swapped if side else own_points, value))
        weights = jnp.concatenate(
            [
                near[:, 2 * PAIR * p : 2 * PAIR * p + PAIR],
                near[:, 2 * PAIR * p + PAIR : 2 * PAIR * (p + 1)],
            ],
            axis=0,
        )
        near_out = mm_t(jnp.concatenate(inputs, axis=0), weights)
        base[:, lanes] = out[0:NRHS] + jnp.where(low16, near_out[0:NRHS], near_out[NRHS:])
        lift[:, lanes] = out[NRHS:]


def half_tile(array, index):
    pair = array[:, pl.ds(pl.multiple_of(PAIR * (index // 2), PAIR), PAIR)]
    lane = lax.broadcasted_iota(jnp.int32, (NRHS, PAIR), 1)
    return pair, lax.shift_right_logical(lane, RANK.bit_length() - 1) == index % 2


def twice(x):
    return jnp.concatenate([x, x], axis=1)


def top_kernel(
    grp_count,
    dev_count,
    start,
    bits,
    record_spans,
    grp_transfer,
    grp_coupling,
    dev_transfer,
    dev_coupling,
    base,
    lift,
    *refs,
):
    blocks = refs[: 2**bits]
    refs = refs[2**bits :]
    earlier = refs[: len(record_spans)]
    product, root, stack, records, d, a, m, inv = refs[len(record_spans) :]
    level = 0
    for ref, span in zip(earlier, record_spans):
        for r in range(2 * span):
            records[2 * level + r] = ref[r]
        level += span
    top = climb(
        blocks, lax.axis_index("grp"), start, bits, grp_count, grp_transfer, stack, records, level
    )
    levels = level + bits
    for n in range(levels):
        d[pair_rows(n), :] = jnp.concatenate(
            [records[2 * n, 0:RANK], records[2 * n + 1, 0:RANK]], axis=1
        )
    d[pair_rows(levels), :] = twice(top[0:RANK])
    invert_pairs(d, a, m, inv, inv.shape[0] // RANK)
    root_inverse = inv[pair_rows(levels), 0:RANK]
    keep = lax.broadcasted_iota(jnp.int32, (RANK, RANK), 0) >= lax.broadcasted_iota(
        jnp.int32, (RANK, RANK), 1
    )
    root[...] = jnp.where(keep, mm_t(top[0:RANK], root_inverse), 0.0)
    dev_levels = dev_count.bit_length() - 1
    low = low_half(NRHS)
    terms = []
    for n in range(levels):
        if n < dev_levels:
            count, shift, spot = dev_count, n, lax.axis_index("dev")
            transfer, coupling = dev_transfer, dev_coupling
        else:
            count, shift, spot = grp_count, n - dev_levels, lax.axis_index("grp")
            transfer, coupling = grp_transfer, grp_coupling
        index = 2 * count - 2 * (count >> shift) + lax.shift_right_logical(spot, shift)
        factors = inv[pair_rows(n), :]
        other = jnp.where(low, 0.0, twice(records[2 * n + 1, RANK:ROWS]))
        pair, half = half_tile(coupling, index)
        xhat = jnp.where(half, twice(mm_t(other, factors)), 0.0)
        yhat = mm_t(xhat, pair)
        terms.append((mm(yhat, factors)[:, 0:RANK], *half_tile(transfer, index)))
    value = None
    for term, pair, half in reversed(terms):
        value = term if value is None else term + mm_t(jnp.where(half, twice(value), 0.0), pair)
    product[...] = base[...] + mm(value, lift[...])


def vmem(count):
    return [pl.BlockSpec(memory_space=pltpu.VMEM)] * count


def hbm(count):
    return [pl.BlockSpec(memory_space=pltpu.HBM)] * count


def in_hbm(x):
    return pltpu.with_memory_space_constraint(x, pltpu.HBM)


def f32(*shape):
    return jax.ShapeDtypeStruct(shape, jnp.float32)


def params(mib):
    return pltpu.CompilerParams(vmem_limit_bytes=mib * MIB)


def micros(count):
    return pl.CostEstimate(flops=count * 10**9, bytes_accessed=MIB, transcendentals=0)


def exchange(block, axis, start, bits):
    count = lax.axis_size(axis)
    return [block] + [
        lax.ppermute(block, axis, [(i, i ^ (k << start)) for i in range(count)])
        for k in range(1, 2**bits)
    ]


def chunks(levels, first):
    out = []
    start = 0
    while start < levels:
        bits = min(first if start == 0 else 2, levels - start)
        out.append((start, bits))
        start += bits
    return out


def climb_call(blocks, axis, start, bits, count, transfer, carried=()):
    anywhere = [pl.BlockSpec(memory_space=pl.ANY)] * len(carried)
    return pl.pallas_call(
        functools.partial(climb_kernel, axis, start, bits, count),
        out_shape=[f32(ROWS, RANK), f32(2 * bits, ROWS, RANK)] + [f32(*c.shape) for c in carried],
        in_specs=vmem(1 + 2**bits) + anywhere,
        out_specs=vmem(2) + anywhere,
        input_output_aliases={1 + 2**bits + n: 2 + n for n in range(len(carried))},
        scratch_shapes=[pltpu.VMEM((2**bits, ROWS, RANK), jnp.float32)],
        compiler_params=params(8),
        cost_estimate=micros(1),
        name="climb",
    )(transfer, *blocks, *carried)


def local_call(gram, z, rhs, after):
    return pl.pallas_call(
        local_kernel,
        out_shape=[f32(BATCH * RANK, PAIR), f32(NRHS, POINT_SPAN + NODE_SPAN)],
        in_specs=vmem(3) + [pl.BlockSpec(memory_space=pl.ANY)],
        out_specs=vmem(2),
        scratch_shapes=[
            pltpu.VMEM((RANK, RANK, LANES), jnp.float32),
            pltpu.VMEM((RANK, RANK, LANES), jnp.float32),
        ],
        compiler_params=params(24),
        cost_estimate=micros(8),
        name="local_factors",
    )(gram, z, rhs, after)


def shards(
    rhs,
    leaf_basis,
    near_blocks,
    near_partner,
    local_transfer,
    local_coupling,
    far_partner,
    dev_transfer,
    dev_coupling,
    grp_transfer,
    grp_coupling,
):
    dev_count = lax.axis_size("dev")
    grp_count = lax.axis_size("grp")
    gram, z, top = pl.pallas_call(
        gram_kernel,
        out_shape=[f32(BATCH * RANK, PAIR), f32(NRHS, NODE_SPAN), f32(ROWS, RANK)],
        in_specs=hbm(3),
        out_specs=vmem(3),
        scratch_shapes=[
            pltpu.VMEM((LEAF, POINT_SPAN), jnp.float32),
            pltpu.VMEM((NRHS, POINT_SPAN), jnp.float32),
            pltpu.VMEM((RANK, NODE_SPAN), jnp.float32),
            pltpu.SemaphoreType.DMA((3,)),
        ],
        compiler_params=params(16),
        cost_estimate=micros(4),
        name="gram",
    )(in_hbm(leaf_basis), in_hbm(rhs), in_hbm(local_transfer))

    records = []
    spans = []
    carried = ()
    inv = None
    dev_transfer = dev_transfer[0]
    dev_coupling = dev_coupling[0]
    for start, bits in chunks(dev_count.bit_length() - 1, 1):
        blocks = exchange(top, "dev", start, bits)
        if records and inv is None:
            inv, packed = local_call(gram, z, rhs, records[0])
            carried = (packed,)
        top, record, *carried = climb_call(
            blocks, "dev", start, bits, dev_count, dev_transfer, carried
        )
        records.append(record)
        spans.append(bits)
    packed = carried[0]

    both = ("grp", "dev")
    ends = grp_count * dev_count - 1
    twin = lax.ppermute(packed, both, [(i, i ^ 1) for i in range(ends + 1)])
    beside = lax.ppermute(
        packed, both, [(i, ((i + 1) ^ 1) - 1) for i in range(1, ends)]
    )

    window_tiles = 3 * (POINT_SPAN + NODE_SPAN) // PAIR
    base, lift = pl.pallas_call(
        couple_kernel,
        out_shape=[f32(NRHS, POINT_SPAN), f32(RANK, POINT_SPAN)],
        in_specs=hbm(2) + vmem(8),
        out_specs=vmem(2),
        scratch_shapes=[
            pltpu.VMEM((2, window_tiles, NRHS, PAIR), jnp.float32),
            pltpu.SMEM(near_partner.shape, jnp.int32),
            pltpu.SMEM(far_partner.shape, jnp.int32),
            pltpu.SemaphoreType.DMA((2,)),
        ],
        compiler_params=params(24),
        cost_estimate=micros(10),
        name="couple",
    )(
        in_hbm(near_partner),
        in_hbm(far_partner),
        packed,
        twin,
        beside,
        inv,
        local_coupling,
        local_transfer,
        leaf_basis,
        near_blocks,
    )

    grp_chunks = chunks(grp_count.bit_length() - 1, 2)
    for start, bits in grp_chunks[:-1]:
        blocks = exchange(top, "grp", start, bits)
        top, record = climb_call(blocks, "grp", start, bits, grp_count, grp_transfer)
        records.append(record)
        spans.append(bits)
    start, bits = grp_chunks[-1]
    blocks = exchange(top, "grp", start, bits)
    levels = sum(spans) + bits
    batch = 8 * ((levels + 1 + 7) // 8)
    return pl.pallas_call(
        functools.partial(top_kernel, grp_count, dev_count, start, bits, tuple(spans)),
        out_shape=[f32(NRHS, POINT_SPAN), f32(RANK, RANK)],
        in_specs=vmem(6 + len(blocks) + len(records)),
        out_specs=vmem(2),
        scratch_shapes=[
            pltpu.VMEM((2**bits, ROWS, RANK), jnp.float32),
            pltpu.VMEM((2 * levels, ROWS, RANK), jnp.float32),
            pltpu.VMEM((batch * RANK, LANES), jnp.float32),
            pltpu.VMEM((RANK, RANK, LANES), jnp.float32),
            pltpu.VMEM((RANK, RANK, LANES), jnp.float32),
            pltpu.VMEM((batch * RANK, PAIR), jnp.float32),
        ],
        compiler_params=params(24),
        cost_estimate=micros(9),
        name="top",
    )(
        grp_transfer,
        grp_coupling,
        dev_transfer,
        dev_coupling,
        base,
        lift,
        *blocks,
        *records,
    )


def solution(mesh):
    return jax.shard_map(
        shards,
        mesh=mesh,
        in_specs=(
            P(None, ("grp", "dev")),
            P(None, ("grp", "dev")),
            P(None, ("grp", "dev")),
            P(("grp", "dev")),
            P(None, ("grp", "dev")),
            P(None, ("grp", "dev")),
            P(("grp", "dev"), None),
            P("grp", None, None),
            P("grp", None, None),
            P(),
            P(),
        ),
        out_specs=(P(None, ("grp", "dev")), P()),
        check_vma=False,
    )
```

```python
import functools

import jax
import jax.numpy as jnp
from jax import lax
from jax.experimental import pallas as pl
from jax.experimental.pallas import tpu as pltpu
from jax.sharding import PartitionSpec as P

RANK = 64
LEAF = 64
NRHS = 16
LOC = 4
LEAF_DEV = 16
LOCAL_NODES = 30
PAIR = 2 * RANK
LANES = 128
BATCH = 16
ROWS = RANK + NRHS
PAIRS = LOCAL_NODES // 2
POINT_SPAN = LEAF_DEV * LEAF
NODE_SPAN = LOCAL_NODES * RANK
OFFSETS = [2 * LEAF_DEV - 2 * (LEAF_DEV >> level) for level in range(LOC)]
MIB = 1 << 20


def halves(x):
    high = x.astype(jnp.bfloat16)
    return high, (x - high.astype(jnp.float32)).astype(jnp.bfloat16)


def three_pass(a, b, side):
    dot = functools.partial(
        lax.dot_general,
        dimension_numbers=(((1,), (side,)), ((), ())),
        preferred_element_type=jnp.float32,
    )
    a_high, a_low = halves(a)
    b_high, b_low = halves(b)
    if a.shape[1] % LANES:
        return dot(a_high, b_high) + (dot(a_high, b_low) + dot(a_low, b_high))
    return dot(
        jnp.concatenate([a_high, a_low, a_high], axis=1),
        jnp.concatenate([b_high, b_high, b_low], axis=side),
    )


def mm(a, b):
    return three_pass(a, b, 0)


def mm_t(a, b):
    return three_pass(a, b, 1)


def gram_pair(u):
    u_high, u_low = halves(u)
    t_high, t_low = halves(u.T)
    dot = functools.partial(jnp.dot, preferred_element_type=jnp.float32)
    wide = dot(t_high, jnp.concatenate([u_high, u_low], axis=1))
    full = wide[:, 0:PAIR] + (wide[:, PAIR:] + dot(t_low, u_high))
    row = lax.broadcasted_iota(jnp.int32, (PAIR, PAIR), 0) < RANK
    return jnp.where(row == low_half(PAIR), full, 0.0)


def low_half(rows):
    return lax.broadcasted_iota(jnp.int32, (rows, PAIR), 1) < RANK


def swap_halves(x):
    return pltpu.roll(x, RANK, 1)


def spread_pair(pair):
    low = low_half(pair.shape[0])
    return jnp.concatenate([jnp.where(low, pair, 0.0), jnp.where(low, 0.0, pair)], axis=0)


def stack_low(pair):
    low = low_half(pair.shape[0])
    return jnp.concatenate(
        [jnp.where(low, pair, 0.0), jnp.where(low, swap_halves(pair), 0.0)], axis=0
    )


def stack_high(pair):
    low = low_half(pair.shape[0])
    return jnp.concatenate(
        [jnp.where(low, 0.0, swap_halves(pair)), jnp.where(low, 0.0, pair)], axis=0
    )


def factor_batch(a, m):
    blocks = RANK // 8
    sub = lax.broadcasted_iota(jnp.int32, (8, LANES), 0)
    for kb in range(blocks):
        k0 = 8 * kb
        rows = [a[k0 + k, k0:RANK, :] for k in range(8)]
        mrows = []
        for k in range(8):
            unit = (sub == k).astype(jnp.float32)
            mrows.append(jnp.concatenate([m[k0 + k, 0:k0, :], unit], axis=0) if kb else unit)
        for k in range(8):
            scale = lax.rsqrt(rows[k][k : k + 1, :])
            rows[k] = rows[k] * scale
            mrows[k] = mrows[k] * scale
            for k2 in range(k + 1, 8):
                f = rows[k][k2 : k2 + 1, :]
                rows[k2] = rows[k2] - f * rows[k]
                mrows[k2] = mrows[k2] - f * mrows[k]
        for k in range(8):
            a[k0 + k, k0:RANK, :] = rows[k]
            m[k0 + k, 0 : k0 + 8, :] = mrows[k]
        for ib in range(kb + 1, blocks):
            for i in range(8 * ib, 8 * ib + 8):
                acc = a[i, 8 * ib : RANK, :]
                old = m[i, 0:k0, :] if kb else None
                new = None
                for k in range(8):
                    f = a[k0 + k, i : i + 1, :]
                    acc = acc - f * a[k0 + k, 8 * ib : RANK, :]
                    part = f * m[k0 + k, 0 : k0 + 8, :]
                    if kb:
                        old = old - part[0:k0]
                    tail = part[k0 : k0 + 8]
                    new = -tail if new is None else new - tail
                a[i, 8 * ib : RANK, :] = acc
                if kb:
                    m[i, 0:k0, :] = old
                m[i, k0 : k0 + 8, :] = new


def invert_pairs(gram, a, m, inv, count):
    for i in range(RANK):
        rows = gram[pl.ds(i, count, stride=RANK), :]
        both = jnp.concatenate([rows, swap_halves(rows)], axis=0)
        first = i - i % 8
        a[i, first:RANK, 0 : 2 * count] = both[:, 0:RANK].T[first:]
    factor_batch(a, m)
    for i in range(RANK):
        width = i - i % 8 + 8
        rows = m[i, 0:width, 0 : 2 * count].T
        if width < RANK:
            rest = jnp.zeros((2 * count, RANK - width), jnp.float32)
            rows = jnp.concatenate([rows, rest], axis=1)
        inv[pl.ds(i, count, stride=RANK), :] = jnp.concatenate([rows[:count], rows[count:]], axis=1)


def gram_kernel(basis_in, rhs_in, transfer_in, gram, z_out, top, basis, rhs, transfer, sems):
    copies = [
        pltpu.make_async_copy(source, target, sems.at[n])
        for n, (source, target) in enumerate(
            ((basis_in, basis), (rhs_in, rhs), (transfer_in, transfer))
        )
    ]
    for copy in copies:
        copy.start()
    copies[0].wait()
    copies[1].wait()
    blocks = []
    for p in range(LEAF_DEV // 2):
        u = basis[:, pair_lanes(p)]
        blocks.append(
            jnp.concatenate([gram_pair(u), mm(rhs[:, pair_lanes(p)], spread_pair(u))], axis=0)
        )
    copies[2].wait()
    tile = 0
    low = low_half(RANK)
    for level in range(LOC):
        pairs = len(blocks)
        for p in range(pairs):
            gram[pair_rows(tile + p), :] = jnp.where(
                low, blocks[p][0:RANK], blocks[p][RANK:PAIR]
            )
            z_out[:, pair_lanes(tile + p)] = blocks[p][PAIR:]
        fs = [
            (stack_high if p % 2 else stack_low)(transfer[:, pair_lanes(tile + p)])
            for p in range(pairs)
        ]
        hs = [mm(block, f) for block, f in zip(blocks, fs)]
        parents = []
        for q in range((pairs + 1) // 2):
            both = slice(2 * q, 2 * q + 2)
            g = mm(
                jnp.concatenate([f.T for f in fs[both]], axis=1),
                jnp.concatenate([h[0:PAIR] for h in hs[both]], axis=0),
            )
            parents.append(jnp.concatenate([g, sum(h[PAIR:] for h in hs[both])], axis=0))
        tile += pairs
        blocks = parents
    top[0:RANK, :] = blocks[0][0:RANK, 0:RANK]
    top[RANK:ROWS, :] = blocks[0][PAIR:, 0:RANK]


def pair_rows(p):
    return slice(RANK * p, RANK * (p + 1))


def pair_lanes(p):
    return slice(PAIR * p, PAIR * (p + 1))


def local_kernel(gram, z, rhs, after, inv, packed, a, m):
    invert_pairs(gram, a, m, inv, BATCH)
    packed[:, 0:POINT_SPAN] = rhs[...]
    for p in range(PAIRS):
        packed[:, POINT_SPAN + PAIR * p : POINT_SPAN + PAIR * (p + 1)] = mm_t(
            z[:, pair_lanes(p)], spread_pair(inv[pair_rows(p), :])
        )


def merge(nodes, tile, transfer):
    pairs = range(len(nodes) // 2)
    fs = [
        stack_low(transfer[:, pl.ds(pl.multiple_of(PAIR * (tile + p), PAIR), PAIR)]) for p in pairs
    ]
    hs = [
        mm(jnp.concatenate([nodes[2 * p], swap_halves(nodes[2 * p + 1])], axis=0), fs[p])
        for p in pairs
    ]
    gs = [
        mm(f[:, 0:RANK].T, jnp.concatenate([h[0:RANK], h[ROWS : ROWS + RANK]], axis=0))
        for f, h in zip(fs, hs)
    ]
    return [
        jnp.concatenate([g, h[RANK:ROWS] + h[ROWS + RANK :]], axis=0) for g, h in zip(gs, hs)
    ]


def climb(blocks, place, start, bits, count, transfer, stack, records, first_record):
    empty = jnp.zeros((ROWS, RANK), jnp.float32)
    for k, block in enumerate(blocks):
        stack[k] = jnp.concatenate([block[...], empty], axis=1)
    here = lax.shift_right_logical(place, start)
    low = here & (2**bits - 1)
    base = here - low
    nodes = [stack[c ^ low] for c in range(2**bits)]
    for level in range(start, start + bits):
        m = count >> level
        own, sibling = (0, 1) if level == start else (low, low ^ 1)
        records[2 * (first_record + level - start)] = stack[own]
        records[2 * (first_record + level - start) + 1] = stack[sibling]
        tile = (2 * count - 2 * m + base) // 2
        nodes = merge(nodes, tile, transfer)
        low = lax.shift_right_logical(low, 1)
        base = lax.shift_right_logical(base, 1)
        for c, node in enumerate(nodes):
            stack[c] = node
    return nodes[0]


def climb_kernel(axis, start, bits, count, transfer, *refs):
    blocks = refs[: 2**bits]
    top, records = refs[-3 - (len(refs) - 2**bits - 3) // 2 :][:2]
    stack = refs[-1]
    top[...] = climb(blocks, lax.axis_index(axis), start, bits, count, transfer, stack, records, 0)[
        :, 0:RANK
    ]


def own_tile(n, grp_count, dev_count, grp_blocks, dev_blocks):
    dev_levels = dev_count.bit_length() - 1
    if n < dev_levels:
        count, shift, place, blocks = dev_count, n, lax.axis_index("dev"), dev_blocks
    else:
        count, shift, place, blocks = grp_count, n - dev_levels, lax.axis_index("grp"), grp_blocks
    index = 2 * count - 2 * (count >> shift) + lax.shift_right_logical(place, shift)
    pair = blocks[:, pl.ds(pl.multiple_of(PAIR * (index // 2), PAIR), PAIR)]
    lane = lax.broadcasted_iota(jnp.int32, (NRHS, PAIR), 1)
    odd = index % 2
    return pair, lax.shift_right_logical(lane, RANK.bit_length() - 1) == odd, odd == 1


def couple_kernel(
    grp_count,
    dev_count,
    levels,
    near_partner_in,
    far_partner_in,
    own,
    twin,
    beside,
    inv,
    coupling,
    near,
    grp_transfer,
    dev_transfer,
    base,
    terms,
    paths,
    window,
    near_partner,
    far_partner,
    sems,
):
    copies = [
        pltpu.make_async_copy(near_partner_in, near_partner, sems.at[0]),
        pltpu.make_async_copy(far_partner_in, far_partner, sems.at[1]),
    ]
    for copy in copies:
        copy.start()
    packed_tiles = (POINT_SPAN + NODE_SPAN) // PAIR
    point_tiles = POINT_SPAN // PAIR
    starts = [point_tiles + OFFSETS[level] // 2 for level in range(LOC)]
    spans = [(0, point_tiles)] + [(starts[level], (LEAF_DEV >> level) // 2) for level in range(LOC)]
    firsts = []
    slot = 0
    place = lax.axis_index("grp") * lax.axis_size("dev") + lax.axis_index("dev")
    odd = place & 1
    for start, span in spans:
        firsts.append(slot)
        for source, shift in ((beside, odd), (own, None), (twin, 1 - odd)):
            first = slot + span if shift is None else slot + 2 * span * shift
            for t in range(span):
                tile = source[:, PAIR * (start + t) : PAIR * (start + t + 1)]
                window[0, first + t] = tile
                window[1, first + t] = swap_halves(tile)
        slot += 3 * span

    def pick(first, index, parity):
        return window[(index & 1) ^ parity, first + lax.shift_right_logical(index, 1)]

    low16 = low_half(NRHS)
    edges = []
    for n in range(levels - 1):
        pair, _, odd_node = own_tile(n, grp_count, dev_count, grp_transfer, dev_transfer)
        edge = jnp.where(odd_node, swap_halves(pair), pair)
        edges.append(jnp.where(low_half(RANK), edge, 0.0))
    path = None
    for n, edge in enumerate(edges):
        path = edge if path is None else mm(path, jnp.concatenate([edge, edge], axis=0))
        paths[:, RANK * n : RANK * (n + 1)] = path[:, 0:RANK]

    for copy in copies:
        copy.wait()
    coupled = []
    for level in range(LOC):
        m = LEAF_DEV >> level
        for p in range(m // 2):
            node = OFFSETS[level] + 2 * p
            values = []
            for side in range(2):
                index = far_partner[0, node + side] - (place - 1) * m
                values.append(pick(firsts[level + 1], index, side))
            xhat = jnp.where(low16, values[0], values[1])
            coupled.append(mm_t(xhat, spread_pair(coupling[:, pair_lanes(node // 2)])))
    for p, y in enumerate(coupled):
        terms[:, pair_lanes(p)] = mm(y, spread_pair(inv[pair_rows(p), :]))

    for p in range(LEAF_DEV // 2):
        lanes = slice(PAIR * p, PAIR * (p + 1))
        own_points = own[:, lanes]
        swapped = swap_halves(own_points)
        inputs = []
        for side in range(2):
            index = near_partner[2 * p + side] - (place - 1) * LEAF_DEV
            value = pick(0, index, 1)
            inputs.append(jnp.where(low16, swapped if side else own_points, value))
        weights = jnp.concatenate(
            [
                near[:, 2 * PAIR * p : 2 * PAIR * p + PAIR],
                near[:, 2 * PAIR * p + PAIR : 2 * PAIR * (p + 1)],
            ],
            axis=0,
        )
        near_out = mm_t(jnp.concatenate(inputs, axis=0), weights)
        base[:, lanes] = jnp.where(low16, near_out[0:NRHS], near_out[NRHS:])


def twice(x):
    return jnp.concatenate([x, x], axis=1)


def top_kernel(
    grp_count,
    dev_count,
    start,
    bits,
    record_spans,
    grp_transfer,
    grp_coupling,
    dev_coupling,
    base,
    terms,
    paths,
    transfer,
    basis,
    *refs,
):
    blocks = refs[: 2**bits]
    refs = refs[2**bits :]
    earlier = refs[: len(record_spans)]
    product, root, stack, records, d, a, m, inv = refs[len(record_spans) :]
    level = 0
    for ref, span in zip(earlier, record_spans):
        for r in range(2 * span):
            records[2 * level + r] = ref[r]
        level += span
    top = climb(
        blocks, lax.axis_index("grp"), start, bits, grp_count, grp_transfer, stack, records, level
    )
    levels = level + bits
    for n in range(levels):
        d[pair_rows(n), :] = jnp.concatenate(
            [records[2 * n, 0:RANK, 0:RANK], records[2 * n + 1, 0:RANK, 0:RANK]], axis=1
        )
    d[pair_rows(levels), :] = top[0:RANK]
    invert_pairs(d, a, m, inv, inv.shape[0] // RANK)
    root_inverse = inv[pair_rows(levels), 0:RANK]
    keep = lax.broadcasted_iota(jnp.int32, (RANK, RANK), 0) >= lax.broadcasted_iota(
        jnp.int32, (RANK, RANK), 1
    )
    root[...] = jnp.where(keep, mm_t(top[0:RANK, 0:RANK], root_inverse), 0.0)
    low = low_half(NRHS)
    xhats = [
        mm_t(
            jnp.where(low, 0.0, swap_halves(records[2 * n + 1, RANK:ROWS])), inv[pair_rows(n), :]
        )
        for n in range(levels)
    ]
    yhats = []
    for n in range(levels):
        pair, half, _ = own_tile(n, grp_count, dev_count, grp_coupling, dev_coupling)
        yhats.append(mm_t(jnp.where(half, twice(xhats[n]), 0.0), pair))
    values = [mm(yhats[n], inv[pair_rows(n), :])[:, 0:RANK] for n in range(levels)]
    value = values[0]
    if levels > 1:
        upper = values[1:]
        edges = paths[...]
        if len(upper) % 2:
            upper.append(jnp.zeros_like(value))
            edges = jnp.concatenate([edges, jnp.zeros_like(edges[:, 0:RANK])], axis=1)
        value = value + mm_t(jnp.concatenate(upper, axis=1), edges)
    state = [twice(value)]
    for level in reversed(range(LOC)):
        m = LEAF_DEV >> level
        tile = OFFSETS[level] // 2
        state = [
            terms[:, pair_lanes(tile + p)]
            + mm_t(
                state[p // 2],
                (stack_high if p % 2 else stack_low)(transfer[:, pair_lanes(tile + p)]),
            )
            for p in range(m // 2)
        ]
    for p in range(LEAF_DEV // 2):
        product[:, pair_lanes(p)] = base[:, pair_lanes(p)] + mm_t(
            state[p], spread_pair(basis[:, pair_lanes(p)])
        )


def vmem(count):
    return [pl.BlockSpec(memory_space=pltpu.VMEM)] * count


def hbm(count):
    return [pl.BlockSpec(memory_space=pltpu.HBM)] * count


def in_hbm(x):
    return pltpu.with_memory_space_constraint(x, pltpu.HBM)


def f32(*shape):
    return jax.ShapeDtypeStruct(shape, jnp.float32)


def params(mib):
    return pltpu.CompilerParams(vmem_limit_bytes=mib * MIB)


def micros(count):
    return pl.CostEstimate(flops=count * 10**9, bytes_accessed=MIB, transcendentals=0)


def exchange(block, axis, start, bits):
    count = lax.axis_size(axis)
    return [block] + [
        lax.ppermute(block, axis, [(i, i ^ (k << start)) for i in range(count)])
        for k in range(1, 2**bits)
    ]


def chunks(levels, first):
    out = []
    start = 0
    while start < levels:
        bits = min(first if start == 0 else 2, levels - start)
        out.append((start, bits))
        start += bits
    return out


def climb_call(blocks, axis, start, bits, count, transfer, carried=()):
    anywhere = [pl.BlockSpec(memory_space=pl.ANY)] * len(carried)
    return pl.pallas_call(
        functools.partial(climb_kernel, axis, start, bits, count),
        out_shape=[f32(ROWS, RANK), f32(2 * bits, ROWS, PAIR)] + [f32(*c.shape) for c in carried],
        in_specs=vmem(1 + 2**bits) + anywhere,
        out_specs=vmem(2) + anywhere,
        input_output_aliases={1 + 2**bits + n: 2 + n for n in range(len(carried))},
        scratch_shapes=[pltpu.VMEM((2**bits, ROWS, PAIR), jnp.float32)],
        compiler_params=params(8),
        cost_estimate=micros(1),
        name="climb",
    )(transfer, *blocks, *carried)


def local_call(gram, z, rhs, after):
    return pl.pallas_call(
        local_kernel,
        out_shape=[f32(BATCH * RANK, PAIR), f32(NRHS, POINT_SPAN + NODE_SPAN)],
        in_specs=vmem(3) + [pl.BlockSpec(memory_space=pl.ANY)],
        out_specs=vmem(2),
        scratch_shapes=[
            pltpu.VMEM((RANK, RANK, LANES), jnp.float32),
            pltpu.VMEM((RANK, RANK, LANES), jnp.float32),
        ],
        compiler_params=params(24),
        cost_estimate=micros(8),
        name="local_factors",
    )(gram, z, rhs, after)


def shards(
    rhs,
    leaf_basis,
    near_blocks,
    near_partner,
    local_transfer,
    local_coupling,
    far_partner,
    dev_transfer,
    dev_coupling,
    grp_transfer,
    grp_coupling,
):
    dev_count = lax.axis_size("dev")
    grp_count = lax.axis_size("grp")
    gram, z, top = pl.pallas_call(
        gram_kernel,
        out_shape=[f32(BATCH * RANK, PAIR), f32(NRHS, NODE_SPAN), f32(ROWS, RANK)],
        in_specs=hbm(3),
        out_specs=vmem(3),
        scratch_shapes=[
            pltpu.VMEM((LEAF, POINT_SPAN), jnp.float32),
            pltpu.VMEM((NRHS, POINT_SPAN), jnp.float32),
            pltpu.VMEM((RANK, NODE_SPAN), jnp.float32),
            pltpu.SemaphoreType.DMA((3,)),
        ],
        compiler_params=params(16),
        cost_estimate=micros(4),
        name="gram",
    )(in_hbm(leaf_basis), in_hbm(rhs), in_hbm(local_transfer))

    records = []
    spans = []
    carried = ()
    inv = None
    dev_transfer = dev_transfer[0]
    dev_coupling = dev_coupling[0]
    for start, bits in chunks(dev_count.bit_length() - 1, 1):
        blocks = exchange(top, "dev", start, bits)
        if records and inv is None:
            inv, packed = local_call(gram, z, rhs, records[0])
            carried = (packed,)
        top, record, *carried = climb_call(
            blocks, "dev", start, bits, dev_count, dev_transfer, carried
        )
        records.append(record)
        spans.append(bits)
    packed = carried[0]

    both = ("grp", "dev")
    ends = grp_count * dev_count - 1
    twin = lax.ppermute(packed, both, [(i, i ^ 1) for i in range(ends + 1)])
    beside = lax.ppermute(
        packed, both, [(i, ((i + 1) ^ 1) - 1) for i in range(1, ends)]
    )

    grp_chunks = chunks(grp_count.bit_length() - 1, 2)
    levels = sum(spans) + grp_count.bit_length() - 1
    window_tiles = 3 * (POINT_SPAN + NODE_SPAN) // PAIR
    base, terms, paths = pl.pallas_call(
        functools.partial(couple_kernel, grp_count, dev_count, levels),
        out_shape=[
            f32(NRHS, POINT_SPAN),
            f32(NRHS, NODE_SPAN),
            f32(RANK, RANK * (levels - 1)),
        ],
        in_specs=hbm(2) + vmem(8),
        out_specs=vmem(3),
        scratch_shapes=[
            pltpu.VMEM((2, window_tiles, NRHS, PAIR), jnp.float32),
            pltpu.SMEM(near_partner.shape, jnp.int32),
            pltpu.SMEM(far_partner.shape, jnp.int32),
            pltpu.SemaphoreType.DMA((2,)),
        ],
        compiler_params=params(24),
        cost_estimate=micros(4),
        name="couple",
    )(
        in_hbm(near_partner),
        in_hbm(far_partner),
        packed,
        twin,
        beside,
        inv,
        local_coupling,
        near_blocks,
        grp_transfer,
        dev_transfer,
    )

    for start, bits in grp_chunks[:-1]:
        blocks = exchange(top, "grp", start, bits)
        top, record = climb_call(blocks, "grp", start, bits, grp_count, grp_transfer)
        records.append(record)
        spans.append(bits)
    start, bits = grp_chunks[-1]
    blocks = exchange(top, "grp", start, bits)
    batch = 8 * ((levels + 1 + 7) // 8)
    return pl.pallas_call(
        functools.partial(top_kernel, grp_count, dev_count, start, bits, tuple(spans)),
        out_shape=[f32(NRHS, POINT_SPAN), f32(RANK, RANK)],
        in_specs=vmem(8 + len(blocks) + len(records)),
        out_specs=vmem(2),
        scratch_shapes=[
            pltpu.VMEM((2**bits, ROWS, PAIR), jnp.float32),
            pltpu.VMEM((2 * levels, ROWS, PAIR), jnp.float32),
            pltpu.VMEM((batch * RANK, LANES), jnp.float32),
            pltpu.VMEM((RANK, RANK, LANES), jnp.float32),
            pltpu.VMEM((RANK, RANK, LANES), jnp.float32),
            pltpu.VMEM((batch * RANK, PAIR), jnp.float32),
        ],
        compiler_params=params(24),
        cost_estimate=micros(9),
        name="top",
    )(
        grp_transfer,
        grp_coupling,
        dev_coupling,
        base,
        terms,
        paths,
        local_transfer,
        leaf_basis,
        *blocks,
        *records,
    )


def solution(mesh):
    return jax.shard_map(
        shards,
        mesh=mesh,
        in_specs=(
            P(None, ("grp", "dev")),
            P(None, ("grp", "dev")),
            P(None, ("grp", "dev")),
            P(("grp", "dev")),
            P(None, ("grp", "dev")),
            P(None, ("grp", "dev")),
            P(("grp", "dev"), None),
            P("grp", None, None),
            P("grp", None, None),
            P(),
            P(),
        ),
        out_specs=(P(None, ("grp", "dev")), P()),
        check_vma=False,
    )
```

```python
import functools

import jax
import jax.numpy as jnp
from jax import lax
from jax.experimental import pallas as pl
from jax.experimental.pallas import tpu as pltpu
from jax.sharding import PartitionSpec as P

RANK = 64
LEAF = 64
NRHS = 16
LOC = 4
LEAF_DEV = 16
LOCAL_NODES = 30
PAIR = 2 * RANK
LANES = 128
BATCH = 16
ROWS = RANK + NRHS
PAIRS = LOCAL_NODES // 2
POINT_SPAN = LEAF_DEV * LEAF
NODE_SPAN = LOCAL_NODES * RANK
OFFSETS = [2 * LEAF_DEV - 2 * (LEAF_DEV >> level) for level in range(LOC)]
MIB = 1 << 20


def halves(x):
    high = x.astype(jnp.bfloat16)
    return high, (x - high.astype(jnp.float32)).astype(jnp.bfloat16)


def three_pass(a, b, side):
    dot = functools.partial(
        lax.dot_general,
        dimension_numbers=(((1,), (side,)), ((), ())),
        preferred_element_type=jnp.float32,
    )
    a_high, a_low = halves(a)
    b_high, b_low = halves(b)
    if a.shape[1] % LANES:
        return dot(a_high, b_high) + (dot(a_high, b_low) + dot(a_low, b_high))
    return dot(
        jnp.concatenate([a_high, a_low, a_high], axis=1),
        jnp.concatenate([b_high, b_high, b_low], axis=side),
    )


def mm(a, b):
    return three_pass(a, b, 0)


def mm_t(a, b):
    return three_pass(a, b, 1)


def gram_pair(u):
    u_high, u_low = halves(u)
    t_high, t_low = halves(u.T)
    dot = functools.partial(jnp.dot, preferred_element_type=jnp.float32)
    wide = dot(t_high, jnp.concatenate([u_high, u_low], axis=1))
    full = wide[:, 0:PAIR] + (wide[:, PAIR:] + dot(t_low, u_high))
    row = lax.broadcasted_iota(jnp.int32, (PAIR, PAIR), 0) < RANK
    return jnp.where(row == low_half(PAIR), full, 0.0)


def low_half(rows):
    return lax.broadcasted_iota(jnp.int32, (rows, PAIR), 1) < RANK


def swap_halves(x):
    return pltpu.roll(x, RANK, 1)


def spread_pair(pair):
    low = low_half(pair.shape[0])
    return jnp.concatenate([jnp.where(low, pair, 0.0), jnp.where(low, 0.0, pair)], axis=0)


def stack_low(pair):
    low = low_half(pair.shape[0])
    return jnp.concatenate(
        [jnp.where(low, pair, 0.0), jnp.where(low, swap_halves(pair), 0.0)], axis=0
    )


def stack_high(pair):
    low = low_half(pair.shape[0])
    return jnp.concatenate(
        [jnp.where(low, 0.0, swap_halves(pair)), jnp.where(low, 0.0, pair)], axis=0
    )


def factor_batch(a, m):
    blocks = RANK // 8
    sub = lax.broadcasted_iota(jnp.int32, (8, LANES), 0)
    for kb in range(blocks):
        k0 = 8 * kb
        rows = [a[k0 + k, k0:RANK, :] for k in range(8)]
        mrows = []
        for k in range(8):
            unit = (sub == k).astype(jnp.float32)
            mrows.append(jnp.concatenate([m[k0 + k, 0:k0, :], unit], axis=0) if kb else unit)
        for k in range(8):
            scale = lax.rsqrt(rows[k][k : k + 1, :])
            rows[k] = rows[k] * scale
            mrows[k] = mrows[k] * scale
            for k2 in range(k + 1, 8):
                f = rows[k][k2 : k2 + 1, :]
                rows[k2] = rows[k2] - f * rows[k]
                mrows[k2] = mrows[k2] - f * mrows[k]
        for k in range(8):
            a[k0 + k, k0:RANK, :] = rows[k]
            m[k0 + k, 0 : k0 + 8, :] = mrows[k]
        for ib in range(kb + 1, blocks):
            for i in range(8 * ib, 8 * ib + 8):
                acc = a[i, 8 * ib : RANK, :]
                old = m[i, 0:k0, :] if kb else None
                new = None
                for k in range(8):
                    f = a[k0 + k, i : i + 1, :]
                    acc = acc - f * a[k0 + k, 8 * ib : RANK, :]
                    part = f * m[k0 + k, 0 : k0 + 8, :]
                    if kb:
                        old = old - part[0:k0]
                    tail = part[k0 : k0 + 8]
                    new = -tail if new is None else new - tail
                a[i, 8 * ib : RANK, :] = acc
                if kb:
                    m[i, 0:k0, :] = old
                m[i, k0 : k0 + 8, :] = new


def invert_pairs(gram, a, m, inv, count):
    for i in range(RANK):
        rows = gram[pl.ds(i, count, stride=RANK), :]
        both = jnp.concatenate([rows, swap_halves(rows)], axis=0)
        first = i - i % 8
        a[i, first:RANK, 0 : 2 * count] = both[:, 0:RANK].T[first:]
    factor_batch(a, m)
    for i in range(RANK):
        width = i - i % 8 + 8
        rows = m[i, 0:width, 0 : 2 * count].T
        if width < RANK:
            rest = jnp.zeros((2 * count, RANK - width), jnp.float32)
            rows = jnp.concatenate([rows, rest], axis=1)
        inv[pl.ds(i, count, stride=RANK), :] = jnp.concatenate([rows[:count], rows[count:]], axis=1)


def gram_kernel(basis_in, rhs_in, transfer_in, gram, z_out, top, basis, rhs, transfer, sems):
    copies = [
        pltpu.make_async_copy(source, target, sems.at[n])
        for n, (source, target) in enumerate(
            ((basis_in, basis), (rhs_in, rhs), (transfer_in, transfer))
        )
    ]
    for copy in copies:
        copy.start()
    copies[0].wait()
    copies[1].wait()
    blocks = []
    for p in range(LEAF_DEV // 2):
        u = basis[:, pair_lanes(p)]
        blocks.append(
            jnp.concatenate([gram_pair(u), mm(rhs[:, pair_lanes(p)], spread_pair(u))], axis=0)
        )
    copies[2].wait()
    tile = 0
    low = low_half(RANK)
    for level in range(LOC):
        pairs = len(blocks)
        for p in range(pairs):
            gram[pair_rows(tile + p), :] = jnp.where(
                low, blocks[p][0:RANK], blocks[p][RANK:PAIR]
            )
            z_out[:, pair_lanes(tile + p)] = blocks[p][PAIR:]
        fs = [
            (stack_high if p % 2 else stack_low)(transfer[:, pair_lanes(tile + p)])
            for p in range(pairs)
        ]
        hs = [mm(block, f) for block, f in zip(blocks, fs)]
        parents = []
        for q in range((pairs + 1) // 2):
            both = slice(2 * q, 2 * q + 2)
            g = mm(
                jnp.concatenate([f.T for f in fs[both]], axis=1),
                jnp.concatenate([h[0:PAIR] for h in hs[both]], axis=0),
            )
            parents.append(jnp.concatenate([g, sum(h[PAIR:] for h in hs[both])], axis=0))
        tile += pairs
        blocks = parents
    top[0:RANK, :] = blocks[0][0:RANK, 0:RANK]
    top[RANK:ROWS, :] = blocks[0][PAIR:, 0:RANK]


def pair_rows(p):
    return slice(RANK * p, RANK * (p + 1))


def pair_lanes(p):
    return slice(PAIR * p, PAIR * (p + 1))


def local_kernel(gram, z, rhs, after, inv, packed, a, m):
    invert_pairs(gram, a, m, inv, BATCH)
    packed[:, 0:POINT_SPAN] = rhs[...]
    for p in range(PAIRS):
        packed[:, POINT_SPAN + PAIR * p : POINT_SPAN + PAIR * (p + 1)] = mm_t(
            z[:, pair_lanes(p)], spread_pair(inv[pair_rows(p), :])
        )


def merge(nodes, tile, transfer):
    pairs = range(len(nodes) // 2)
    fs = [
        stack_low(transfer[:, pl.ds(pl.multiple_of(PAIR * (tile + p), PAIR), PAIR)]) for p in pairs
    ]
    hs = [
        mm(jnp.concatenate([nodes[2 * p], swap_halves(nodes[2 * p + 1])], axis=0), fs[p])
        for p in pairs
    ]
    gs = [
        mm(f[:, 0:RANK].T, jnp.concatenate([h[0:RANK], h[ROWS : ROWS + RANK]], axis=0))
        for f, h in zip(fs, hs)
    ]
    return [
        jnp.concatenate([g, h[RANK:ROWS] + h[ROWS + RANK :]], axis=0) for g, h in zip(gs, hs)
    ]


def climb(blocks, place, start, bits, count, transfer, stack, records, first_record):
    empty = jnp.zeros((ROWS, RANK), jnp.float32)
    for k, block in enumerate(blocks):
        stack[k] = jnp.concatenate([block[...], empty], axis=1)
    here = lax.shift_right_logical(place, start)
    low = here & (2**bits - 1)
    base = here - low
    nodes = [stack[c ^ low] for c in range(2**bits)]
    for level in range(start, start + bits):
        m = count >> level
        own, sibling = (0, 1) if level == start else (low, low ^ 1)
        records[2 * (first_record + level - start)] = stack[own]
        records[2 * (first_record + level - start) + 1] = stack[sibling]
        tile = (2 * count - 2 * m + base) // 2
        nodes = merge(nodes, tile, transfer)
        low = lax.shift_right_logical(low, 1)
        base = lax.shift_right_logical(base, 1)
        for c, node in enumerate(nodes):
            stack[c] = node
    return nodes[0]


def climb_kernel(axis, start, bits, count, transfer, *refs):
    blocks = refs[: 2**bits]
    top, records = refs[-3 - (len(refs) - 2**bits - 3) // 2 :][:2]
    stack = refs[-1]
    top[...] = climb(blocks, lax.axis_index(axis), start, bits, count, transfer, stack, records, 0)[
        :, 0:RANK
    ]


def own_tile(n, grp_count, dev_count, grp_blocks, dev_blocks):
    dev_levels = dev_count.bit_length() - 1
    if n < dev_levels:
        count, shift, place, blocks = dev_count, n, lax.axis_index("dev"), dev_blocks
    else:
        count, shift, place, blocks = grp_count, n - dev_levels, lax.axis_index("grp"), grp_blocks
    index = 2 * count - 2 * (count >> shift) + lax.shift_right_logical(place, shift)
    pair = blocks[:, pl.ds(pl.multiple_of(PAIR * (index // 2), PAIR), PAIR)]
    lane = lax.broadcasted_iota(jnp.int32, (NRHS, PAIR), 1)
    odd = index % 2
    return pair, lax.shift_right_logical(lane, RANK.bit_length() - 1) == odd, odd == 1


def couple_kernel(
    near_partner_in,
    far_partner_in,
    own,
    twin,
    beside,
    inv,
    root_value,
    coupling,
    transfer,
    basis,
    near,
    product,
    window,
    near_partner,
    far_partner,
    sems,
):
    copies = [
        pltpu.make_async_copy(near_partner_in, near_partner, sems.at[0]),
        pltpu.make_async_copy(far_partner_in, far_partner, sems.at[1]),
    ]
    for copy in copies:
        copy.start()
    packed_tiles = (POINT_SPAN + NODE_SPAN) // PAIR
    point_tiles = POINT_SPAN // PAIR
    starts = [point_tiles + OFFSETS[level] // 2 for level in range(LOC)]
    spans = [(0, point_tiles)] + [(starts[level], (LEAF_DEV >> level) // 2) for level in range(LOC)]
    firsts = []
    slot = 0
    place = lax.axis_index("grp") * lax.axis_size("dev") + lax.axis_index("dev")
    odd = place & 1
    for start, span in spans:
        firsts.append(slot)
        for source, shift in ((beside, odd), (own, None), (twin, 1 - odd)):
            first = slot + span if shift is None else slot + 2 * span * shift
            for t in range(span):
                tile = source[:, PAIR * (start + t) : PAIR * (start + t + 1)]
                window[0, first + t] = tile
                window[1, first + t] = swap_halves(tile)
        slot += 3 * span

    def pick(first, index, parity):
        return window[(index & 1) ^ parity, first + lax.shift_right_logical(index, 1)]

    low16 = low_half(NRHS)
    for copy in copies:
        copy.wait()
    coupled = []
    for level in range(LOC):
        m = LEAF_DEV >> level
        for p in range(m // 2):
            node = OFFSETS[level] + 2 * p
            values = []
            for side in range(2):
                index = far_partner[0, node + side] - (place - 1) * m
                values.append(pick(firsts[level + 1], index, side))
            xhat = jnp.where(low16, values[0], values[1])
            coupled.append(mm_t(xhat, spread_pair(coupling[:, pair_lanes(node // 2)])))
    terms = [mm(y, spread_pair(inv[pair_rows(p), :])) for p, y in enumerate(coupled)]
    nears = []
    for p in range(LEAF_DEV // 2):
        lanes = slice(PAIR * p, PAIR * (p + 1))
        own_points = own[:, lanes]
        swapped = swap_halves(own_points)
        inputs = []
        for side in range(2):
            index = near_partner[2 * p + side] - (place - 1) * LEAF_DEV
            value = pick(0, index, 1)
            inputs.append(jnp.where(low16, swapped if side else own_points, value))
        weights = jnp.concatenate(
            [
                near[:, 2 * PAIR * p : 2 * PAIR * p + PAIR],
                near[:, 2 * PAIR * p + PAIR : 2 * PAIR * (p + 1)],
            ],
            axis=0,
        )
        near_out = mm_t(jnp.concatenate(inputs, axis=0), weights)
        nears.append(jnp.where(low16, near_out[0:NRHS], near_out[NRHS:]))
    state = [twice(root_value[...])]
    for level in reversed(range(LOC)):
        m = LEAF_DEV >> level
        tile = OFFSETS[level] // 2
        state = [
            terms[tile + p]
            + mm_t(
                state[p // 2],
                (stack_high if p % 2 else stack_low)(transfer[:, pair_lanes(tile + p)]),
            )
            for p in range(m // 2)
        ]
    for p in range(LEAF_DEV // 2):
        product[:, pair_lanes(p)] = nears[p] + mm_t(
            state[p], spread_pair(basis[:, pair_lanes(p)])
        )


def twice(x):
    return jnp.concatenate([x, x], axis=1)


def top_kernel(
    grp_count,
    dev_count,
    start,
    bits,
    record_spans,
    grp_transfer,
    grp_coupling,
    dev_transfer,
    dev_coupling,
    *refs,
):
    blocks = refs[: 2**bits]
    refs = refs[2**bits :]
    earlier = refs[: len(record_spans)]
    value_out, root, stack, records, d, a, m, inv = refs[len(record_spans) :]
    level = 0
    for ref, span in zip(earlier, record_spans):
        for r in range(2 * span):
            records[2 * level + r] = ref[r]
        level += span
    top = climb(
        blocks, lax.axis_index("grp"), start, bits, grp_count, grp_transfer, stack, records, level
    )
    levels = level + bits
    edges = []
    for n in range(levels - 1):
        pair, _, odd_node = own_tile(n, grp_count, dev_count, grp_transfer, dev_transfer)
        edge = jnp.where(odd_node, swap_halves(pair), pair)
        edges.append(jnp.where(low_half(RANK), edge, 0.0))
    path = None
    paths = []
    for n, edge in enumerate(edges):
        path = edge if path is None else mm(path, jnp.concatenate([edge, edge], axis=0))
        paths.append(path[:, 0:RANK])
    for n in range(levels):
        d[pair_rows(n), :] = jnp.concatenate(
            [records[2 * n, 0:RANK, 0:RANK], records[2 * n + 1, 0:RANK, 0:RANK]], axis=1
        )
    d[pair_rows(levels), :] = top[0:RANK]
    invert_pairs(d, a, m, inv, inv.shape[0] // RANK)
    root_inverse = inv[pair_rows(levels), 0:RANK]
    keep = lax.broadcasted_iota(jnp.int32, (RANK, RANK), 0) >= lax.broadcasted_iota(
        jnp.int32, (RANK, RANK), 1
    )
    root[...] = jnp.where(keep, mm_t(top[0:RANK, 0:RANK], root_inverse), 0.0)
    low = low_half(NRHS)
    xhats = [
        mm_t(
            jnp.where(low, 0.0, swap_halves(records[2 * n + 1, RANK:ROWS])), inv[pair_rows(n), :]
        )
        for n in range(levels)
    ]
    yhats = []
    for n in range(levels):
        pair, half, _ = own_tile(n, grp_count, dev_count, grp_coupling, dev_coupling)
        yhats.append(mm_t(jnp.where(half, twice(xhats[n]), 0.0), pair))
    values = [mm(yhats[n], inv[pair_rows(n), :])[:, 0:RANK] for n in range(levels)]
    value = values[0]
    if levels > 1:
        upper = values[1:]
        if len(upper) % 2:
            upper.append(jnp.zeros_like(value))
            paths.append(jnp.zeros_like(paths[0]))
        value = value + mm_t(jnp.concatenate(upper, axis=1), jnp.concatenate(paths, axis=1))
    value_out[...] = value


def vmem(count):
    return [pl.BlockSpec(memory_space=pltpu.VMEM)] * count


def hbm(count):
    return [pl.BlockSpec(memory_space=pltpu.HBM)] * count


def in_hbm(x):
    return pltpu.with_memory_space_constraint(x, pltpu.HBM)


def f32(*shape):
    return jax.ShapeDtypeStruct(shape, jnp.float32)


def params(mib):
    return pltpu.CompilerParams(vmem_limit_bytes=mib * MIB)


def micros(count):
    return pl.CostEstimate(flops=count * 10**9, bytes_accessed=MIB, transcendentals=0)


def exchange(block, axis, start, bits):
    count = lax.axis_size(axis)
    return [block] + [
        lax.ppermute(block, axis, [(i, i ^ (k << start)) for i in range(count)])
        for k in range(1, 2**bits)
    ]


def chunks(levels, first):
    out = []
    start = 0
    while start < levels:
        bits = min(first if start == 0 else 2, levels - start)
        out.append((start, bits))
        start += bits
    return out


def climb_call(blocks, axis, start, bits, count, transfer, carried=()):
    anywhere = [pl.BlockSpec(memory_space=pl.ANY)] * len(carried)
    return pl.pallas_call(
        functools.partial(climb_kernel, axis, start, bits, count),
        out_shape=[f32(ROWS, RANK), f32(2 * bits, ROWS, PAIR)] + [f32(*c.shape) for c in carried],
        in_specs=vmem(1 + 2**bits) + anywhere,
        out_specs=vmem(2) + anywhere,
        input_output_aliases={1 + 2**bits + n: 2 + n for n in range(len(carried))},
        scratch_shapes=[pltpu.VMEM((2**bits, ROWS, PAIR), jnp.float32)],
        compiler_params=params(8),
        cost_estimate=micros(1),
        name="climb",
    )(transfer, *blocks, *carried)


def local_call(gram, z, rhs, after):
    return pl.pallas_call(
        local_kernel,
        out_shape=[f32(BATCH * RANK, PAIR), f32(NRHS, POINT_SPAN + NODE_SPAN)],
        in_specs=vmem(3) + [pl.BlockSpec(memory_space=pl.ANY)],
        out_specs=vmem(2),
        scratch_shapes=[
            pltpu.VMEM((RANK, RANK, LANES), jnp.float32),
            pltpu.VMEM((RANK, RANK, LANES), jnp.float32),
        ],
        compiler_params=params(24),
        cost_estimate=micros(8),
        name="local_factors",
    )(gram, z, rhs, after)


def shards(
    rhs,
    leaf_basis,
    near_blocks,
    near_partner,
    local_transfer,
    local_coupling,
    far_partner,
    dev_transfer,
    dev_coupling,
    grp_transfer,
    grp_coupling,
):
    dev_count = lax.axis_size("dev")
    grp_count = lax.axis_size("grp")
    gram, z, top = pl.pallas_call(
        gram_kernel,
        out_shape=[f32(BATCH * RANK, PAIR), f32(NRHS, NODE_SPAN), f32(ROWS, RANK)],
        in_specs=hbm(3),
        out_specs=vmem(3),
        scratch_shapes=[
            pltpu.VMEM((LEAF, POINT_SPAN), jnp.float32),
            pltpu.VMEM((NRHS, POINT_SPAN), jnp.float32),
            pltpu.VMEM((RANK, NODE_SPAN), jnp.float32),
            pltpu.SemaphoreType.DMA((3,)),
        ],
        compiler_params=params(16),
        cost_estimate=micros(4),
        name="gram",
    )(in_hbm(leaf_basis), in_hbm(rhs), in_hbm(local_transfer))

    records = []
    spans = []
    carried = ()
    inv = None
    dev_transfer = dev_transfer[0]
    dev_coupling = dev_coupling[0]
    for start, bits in chunks(dev_count.bit_length() - 1, 1):
        blocks = exchange(top, "dev", start, bits)
        if records and inv is None:
            inv, packed = local_call(gram, z, rhs, records[0])
            carried = (packed,)
        top, record, *carried = climb_call(
            blocks, "dev", start, bits, dev_count, dev_transfer, carried
        )
        records.append(record)
        spans.append(bits)
    packed = carried[0]

    both = ("grp", "dev")
    ends = grp_count * dev_count - 1
    twin = lax.ppermute(packed, both, [(i, i ^ 1) for i in range(ends + 1)])
    pairs = [(i, i + 1) for i in range(1, ends, 2)]
    beside = lax.ppermute(packed, both, pairs + [(j, i) for i, j in pairs])

    grp_chunks = chunks(grp_count.bit_length() - 1, 2)
    levels = sum(spans) + grp_count.bit_length() - 1
    for start, bits in grp_chunks[:-1]:
        blocks = exchange(top, "grp", start, bits)
        top, record = climb_call(blocks, "grp", start, bits, grp_count, grp_transfer)
        records.append(record)
        spans.append(bits)
    start, bits = grp_chunks[-1]
    blocks = exchange(top, "grp", start, bits)
    batch = 8 * ((levels + 1 + 7) // 8)
    value, root = pl.pallas_call(
        functools.partial(top_kernel, grp_count, dev_count, start, bits, tuple(spans)),
        out_shape=[f32(NRHS, RANK), f32(RANK, RANK)],
        in_specs=vmem(4 + len(blocks) + len(records)),
        out_specs=vmem(2),
        scratch_shapes=[
            pltpu.VMEM((2**bits, ROWS, PAIR), jnp.float32),
            pltpu.VMEM((2 * levels, ROWS, PAIR), jnp.float32),
            pltpu.VMEM((batch * RANK, LANES), jnp.float32),
            pltpu.VMEM((RANK, RANK, LANES), jnp.float32),
            pltpu.VMEM((RANK, RANK, LANES), jnp.float32),
            pltpu.VMEM((batch * RANK, PAIR), jnp.float32),
        ],
        compiler_params=params(24),
        cost_estimate=micros(7),
        name="top",
    )(grp_transfer, grp_coupling, dev_transfer, dev_coupling, *blocks, *records)

    window_tiles = 3 * (POINT_SPAN + NODE_SPAN) // PAIR
    product = pl.pallas_call(
        couple_kernel,
        out_shape=f32(NRHS, POINT_SPAN),
        in_specs=hbm(2) + vmem(9),
        out_specs=vmem(1)[0],
        scratch_shapes=[
            pltpu.VMEM((2, window_tiles, NRHS, PAIR), jnp.float32),
            pltpu.SMEM(near_partner.shape, jnp.int32),
            pltpu.SMEM(far_partner.shape, jnp.int32),
            pltpu.SemaphoreType.DMA((2,)),
        ],
        compiler_params=params(24),
        cost_estimate=micros(3),
        name="couple",
    )(
        in_hbm(near_partner),
        in_hbm(far_partner),
        packed,
        twin,
        beside,
        inv,
        value,
        local_coupling,
        local_transfer,
        leaf_basis,
        near_blocks,
    )
    return product, root


def solution(mesh):
    return jax.shard_map(
        shards,
        mesh=mesh,
        in_specs=(
            P(None, ("grp", "dev")),
            P(None, ("grp", "dev")),
            P(None, ("grp", "dev")),
            P(("grp", "dev")),
            P(None, ("grp", "dev")),
            P(None, ("grp", "dev")),
            P(("grp", "dev"), None),
            P("grp", None, None),
            P("grp", None, None),
            P(),
            P(),
        ),
        out_specs=(P(None, ("grp", "dev")), P()),
        check_vma=False,
    )
```

```python
import functools

import jax
import jax.numpy as jnp
from jax import lax
from jax.experimental import pallas as pl
from jax.experimental.pallas import tpu as pltpu
from jax.sharding import PartitionSpec as P

RANK = 64
LEAF = 64
NRHS = 16
LOC = 4
LEAF_DEV = 16
LOCAL_NODES = 30
PAIR = 2 * RANK
LANES = 128
BATCH = 16
ROWS = RANK + NRHS
PAIRS = LOCAL_NODES // 2
POINT_SPAN = LEAF_DEV * LEAF
NODE_SPAN = LOCAL_NODES * RANK
OFFSETS = [2 * LEAF_DEV - 2 * (LEAF_DEV >> level) for level in range(LOC)]
MIB = 1 << 20


def halves(x):
    high = x.astype(jnp.bfloat16)
    return high, (x - high.astype(jnp.float32)).astype(jnp.bfloat16)


def three_pass(a, b, side):
    dot = functools.partial(
        lax.dot_general,
        dimension_numbers=(((1,), (side,)), ((), ())),
        preferred_element_type=jnp.float32,
    )
    a_high, a_low = halves(a)
    b_high, b_low = halves(b)
    if a.shape[1] % LANES:
        return dot(a_high, b_high) + (dot(a_high, b_low) + dot(a_low, b_high))
    return dot(
        jnp.concatenate([a_high, a_low, a_high], axis=1),
        jnp.concatenate([b_high, b_high, b_low], axis=side),
    )


def mm(a, b):
    return three_pass(a, b, 0)


def mm_t(a, b):
    return three_pass(a, b, 1)


def gram_pair(u):
    u_high, u_low = halves(u)
    t_high, t_low = halves(u.T)
    dot = functools.partial(jnp.dot, preferred_element_type=jnp.float32)
    wide = dot(t_high, jnp.concatenate([u_high, u_low], axis=1))
    full = wide[:, 0:PAIR] + (wide[:, PAIR:] + dot(t_low, u_high))
    row = lax.broadcasted_iota(jnp.int32, (PAIR, PAIR), 0) < RANK
    return jnp.where(row == low_half(PAIR), full, 0.0)


def low_half(rows):
    return lax.broadcasted_iota(jnp.int32, (rows, PAIR), 1) < RANK


def swap_halves(x):
    return pltpu.roll(x, RANK, 1)


def spread_pair(pair):
    low = low_half(pair.shape[0])
    return jnp.concatenate([jnp.where(low, pair, 0.0), jnp.where(low, 0.0, pair)], axis=0)


def stack_low(pair):
    low = low_half(pair.shape[0])
    return jnp.concatenate(
        [jnp.where(low, pair, 0.0), jnp.where(low, swap_halves(pair), 0.0)], axis=0
    )


def stack_high(pair):
    low = low_half(pair.shape[0])
    return jnp.concatenate(
        [jnp.where(low, 0.0, swap_halves(pair)), jnp.where(low, 0.0, pair)], axis=0
    )


def factor_batch(a, m):
    blocks = RANK // 8
    sub = lax.broadcasted_iota(jnp.int32, (8, LANES), 0)
    for kb in range(blocks):
        k0 = 8 * kb
        rows = [a[k0 + k, k0:RANK, :] for k in range(8)]
        mrows = []
        for k in range(8):
            unit = (sub == k).astype(jnp.float32)
            mrows.append(jnp.concatenate([m[k0 + k, 0:k0, :], unit], axis=0) if kb else unit)
        for k in range(8):
            scale = lax.rsqrt(rows[k][k : k + 1, :])
            rows[k] = rows[k] * scale
            mrows[k] = mrows[k] * scale
            for k2 in range(k + 1, 8):
                f = rows[k][k2 : k2 + 1, :]
                rows[k2] = rows[k2] - f * rows[k]
                mrows[k2] = mrows[k2] - f * mrows[k]
        for k in range(8):
            a[k0 + k, k0:RANK, :] = rows[k]
            m[k0 + k, 0 : k0 + 8, :] = mrows[k]
        for ib in range(kb + 1, blocks):
            for i in range(8 * ib, 8 * ib + 8):
                acc = a[i, 8 * ib : RANK, :]
                old = m[i, 0:k0, :] if kb else None
                new = None
                for k in range(8):
                    f = a[k0 + k, i : i + 1, :]
                    acc = acc - f * a[k0 + k, 8 * ib : RANK, :]
                    part = f * m[k0 + k, 0 : k0 + 8, :]
                    if kb:
                        old = old - part[0:k0]
                    tail = part[k0 : k0 + 8]
                    new = -tail if new is None else new - tail
                a[i, 8 * ib : RANK, :] = acc
                if kb:
                    m[i, 0:k0, :] = old
                m[i, k0 : k0 + 8, :] = new


def invert_pairs(gram, a, m, inv, count):
    for i in range(RANK):
        rows = gram[pl.ds(i, count, stride=RANK), :]
        both = jnp.concatenate([rows, swap_halves(rows)], axis=0)
        first = i - i % 8
        a[i, first:RANK, 0 : 2 * count] = both[:, 0:RANK].T[first:]
    factor_batch(a, m)
    for i in range(RANK):
        width = i - i % 8 + 8
        rows = m[i, 0:width, 0 : 2 * count].T
        if width < RANK:
            rest = jnp.zeros((2 * count, RANK - width), jnp.float32)
            rows = jnp.concatenate([rows, rest], axis=1)
        inv[pl.ds(i, count, stride=RANK), :] = jnp.concatenate([rows[:count], rows[count:]], axis=1)


def gram_kernel(basis_in, rhs_in, transfer_in, gram, z_out, top, basis, rhs, transfer, sems):
    copies = [
        pltpu.make_async_copy(source, target, sems.at[n])
        for n, (source, target) in enumerate(
            ((basis_in, basis), (rhs_in, rhs), (transfer_in, transfer))
        )
    ]
    for copy in copies:
        copy.start()
    copies[0].wait()
    copies[1].wait()
    blocks = []
    for p in range(LEAF_DEV // 2):
        u = basis[:, pair_lanes(p)]
        blocks.append(
            jnp.concatenate([gram_pair(u), mm(rhs[:, pair_lanes(p)], spread_pair(u))], axis=0)
        )
    copies[2].wait()
    tile = 0
    low = low_half(RANK)
    for level in range(LOC):
        pairs = len(blocks)
        for p in range(pairs):
            gram[pair_rows(tile + p), :] = jnp.where(
                low, blocks[p][0:RANK], blocks[p][RANK:PAIR]
            )
            z_out[:, pair_lanes(tile + p)] = blocks[p][PAIR:]
        fs = [
            (stack_high if p % 2 else stack_low)(transfer[:, pair_lanes(tile + p)])
            for p in range(pairs)
        ]
        hs = [mm(block, f) for block, f in zip(blocks, fs)]
        parents = []
        for q in range((pairs + 1) // 2):
            both = slice(2 * q, 2 * q + 2)
            g = mm(
                jnp.concatenate([f.T for f in fs[both]], axis=1),
                jnp.concatenate([h[0:PAIR] for h in hs[both]], axis=0),
            )
            parents.append(jnp.concatenate([g, sum(h[PAIR:] for h in hs[both])], axis=0))
        tile += pairs
        blocks = parents
    top[0:RANK, :] = blocks[0][0:RANK, 0:RANK]
    top[RANK:ROWS, :] = blocks[0][PAIR:, 0:RANK]


def pair_rows(p):
    return slice(RANK * p, RANK * (p + 1))


def pair_lanes(p):
    return slice(PAIR * p, PAIR * (p + 1))


def local_kernel(
    gram, z, rhs, after, near_in, far_in, inv, packed, near_partner, far_partner, a, m, sems
):
    copies = [
        pltpu.make_async_copy(near_in, near_partner, sems.at[0]),
        pltpu.make_async_copy(far_in, far_partner, sems.at[1]),
    ]
    for copy in copies:
        copy.start()
    invert_pairs(gram, a, m, inv, BATCH)
    packed[:, 0:POINT_SPAN] = rhs[...]
    for p in range(PAIRS):
        packed[:, POINT_SPAN + PAIR * p : POINT_SPAN + PAIR * (p + 1)] = mm_t(
            z[:, pair_lanes(p)], spread_pair(inv[pair_rows(p), :])
        )
    for copy in copies:
        copy.wait()


def merge(nodes, tile, transfer):
    pairs = range(len(nodes) // 2)
    fs = [
        stack_low(transfer[:, pl.ds(pl.multiple_of(PAIR * (tile + p), PAIR), PAIR)]) for p in pairs
    ]
    hs = [
        mm(jnp.concatenate([nodes[2 * p], swap_halves(nodes[2 * p + 1])], axis=0), fs[p])
        for p in pairs
    ]
    gs = [
        mm(f[:, 0:RANK].T, jnp.concatenate([h[0:RANK], h[ROWS : ROWS + RANK]], axis=0))
        for f, h in zip(fs, hs)
    ]
    return [
        jnp.concatenate([g, h[RANK:ROWS] + h[ROWS + RANK :]], axis=0) for g, h in zip(gs, hs)
    ]


def climb(blocks, place, start, bits, count, transfer, stack, records, first_record):
    empty = jnp.zeros((ROWS, RANK), jnp.float32)
    for k, block in enumerate(blocks):
        stack[k] = jnp.concatenate([block[...], empty], axis=1)
    here = lax.shift_right_logical(place, start)
    low = here & (2**bits - 1)
    base = here - low
    nodes = [stack[c ^ low] for c in range(2**bits)]
    for level in range(start, start + bits):
        m = count >> level
        own, sibling = (0, 1) if level == start else (low, low ^ 1)
        records[2 * (first_record + level - start)] = stack[own]
        records[2 * (first_record + level - start) + 1] = stack[sibling]
        tile = (2 * count - 2 * m + base) // 2
        nodes = merge(nodes, tile, transfer)
        low = lax.shift_right_logical(low, 1)
        base = lax.shift_right_logical(base, 1)
        for c, node in enumerate(nodes):
            stack[c] = node
    return nodes[0]


def climb_kernel(axis, start, bits, count, transfer, *refs):
    blocks = refs[: 2**bits]
    top, records = refs[-3 - (len(refs) - 2**bits - 3) // 2 :][:2]
    stack = refs[-1]
    top[...] = climb(blocks, lax.axis_index(axis), start, bits, count, transfer, stack, records, 0)[
        :, 0:RANK
    ]


def own_tile(n, grp_count, dev_count, grp_blocks, dev_blocks):
    dev_levels = dev_count.bit_length() - 1
    if n < dev_levels:
        count, shift, place, blocks = dev_count, n, lax.axis_index("dev"), dev_blocks
    else:
        count, shift, place, blocks = grp_count, n - dev_levels, lax.axis_index("grp"), grp_blocks
    index = 2 * count - 2 * (count >> shift) + lax.shift_right_logical(place, shift)
    pair = blocks[:, pl.ds(pl.multiple_of(PAIR * (index // 2), PAIR), PAIR)]
    lane = lax.broadcasted_iota(jnp.int32, (NRHS, PAIR), 1)
    odd = index % 2
    return pair, lax.shift_right_logical(lane, RANK.bit_length() - 1) == odd, odd == 1


def couple_kernel(
    near_partner_in,
    far_partner_in,
    own,
    twin,
    beside,
    inv,
    root_value,
    coupling,
    transfer,
    basis,
    near,
    product,
    window,
    near_partner,
    far_partner,
    sems,
):
    copies = [
        pltpu.make_async_copy(near_partner_in, near_partner, sems.at[0]),
        pltpu.make_async_copy(far_partner_in, far_partner, sems.at[1]),
    ]
    for copy in copies:
        copy.start()
    packed_tiles = (POINT_SPAN + NODE_SPAN) // PAIR
    point_tiles = POINT_SPAN // PAIR
    starts = [point_tiles + OFFSETS[level] // 2 for level in range(LOC)]
    spans = [(0, point_tiles)] + [(starts[level], (LEAF_DEV >> level) // 2) for level in range(LOC)]
    firsts = []
    slot = 0
    place = lax.axis_index("grp") * lax.axis_size("dev") + lax.axis_index("dev")
    odd = place & 1
    for start, span in spans:
        firsts.append(slot)
        for source, shift in ((beside, odd), (own, None), (twin, 1 - odd)):
            first = slot + span if shift is None else slot + 2 * span * shift
            for t in range(span):
                tile = source[:, PAIR * (start + t) : PAIR * (start + t + 1)]
                window[first + t] = tile
        slot += 3 * span

    def pick(first, index, parity):
        tile = window[first + lax.shift_right_logical(index, 1)]
        return jnp.where((index & 1) == parity, tile, swap_halves(tile))

    low16 = low_half(NRHS)
    for copy in copies:
        copy.wait()
    coupled = []
    for level in range(LOC):
        m = LEAF_DEV >> level
        for p in range(m // 2):
            node = OFFSETS[level] + 2 * p
            values = []
            for side in range(2):
                index = far_partner[0, node + side] - (place - 1) * m
                values.append(pick(firsts[level + 1], index, side))
            xhat = jnp.where(low16, values[0], values[1])
            coupled.append(mm_t(xhat, spread_pair(coupling[:, pair_lanes(node // 2)])))

    def terms(level):
        tile = OFFSETS[level] // 2
        return [
            mm(coupled[p], spread_pair(inv[pair_rows(p), :]))
            for p in range(tile, tile + (LEAF_DEV >> level + 1))
        ]

    def near_field(p):
        own_points = own[:, pair_lanes(p)]
        swapped = swap_halves(own_points)
        inputs = []
        for side in range(2):
            index = near_partner[2 * p + side] - (place - 1) * LEAF_DEV
            partner = pick(0, index, 1)
            inputs.append(jnp.where(low16, swapped if side else own_points, partner))
        weights = jnp.concatenate(
            [
                near[:, 2 * PAIR * p : 2 * PAIR * p + PAIR],
                near[:, 2 * PAIR * p + PAIR : 2 * PAIR * (p + 1)],
            ],
            axis=0,
        )
        out = mm_t(jnp.concatenate(inputs, axis=0), weights)
        return jnp.where(low16, out[0:NRHS], out[NRHS:])

    nears = []
    state = [twice(root_value[...])]
    ready = terms(LOC - 1)
    for level in reversed(range(LOC)):
        tile = OFFSETS[level] // 2
        pairs = LEAF_DEV >> level + 1
        swept = [
            mm_t(
                state[p // 2],
                (stack_high if p % 2 else stack_low)(transfer[:, pair_lanes(tile + p)]),
            )
            for p in range(pairs)
        ]
        state = [term + value for term, value in zip(ready, swept)]
        if level:
            ready = terms(level - 1)
        nears += [near_field(p) for p in range(2 * len(nears) // 2, 2 * (LOC - level))]
    for p in range(LEAF_DEV // 2):
        product[:, pair_lanes(p)] = nears[p] + mm_t(
            state[p], spread_pair(basis[:, pair_lanes(p)])
        )


def twice(x):
    return jnp.concatenate([x, x], axis=1)


def top_kernel(
    grp_count,
    dev_count,
    start,
    bits,
    record_spans,
    grp_transfer,
    grp_coupling,
    dev_transfer,
    dev_coupling,
    *refs,
):
    blocks = refs[: 2**bits]
    refs = refs[2**bits :]
    earlier = refs[: len(record_spans)]
    value_out, root, stack, records, d, a, m, inv = refs[len(record_spans) :]
    level = 0
    for ref, span in zip(earlier, record_spans):
        for r in range(2 * span):
            records[2 * level + r] = ref[r]
        level += span
    top = climb(
        blocks, lax.axis_index("grp"), start, bits, grp_count, grp_transfer, stack, records, level
    )
    levels = level + bits
    edges = []
    for n in range(levels - 1):
        pair, _, odd_node = own_tile(n, grp_count, dev_count, grp_transfer, dev_transfer)
        edge = jnp.where(odd_node, swap_halves(pair), pair)
        edges.append(jnp.where(low_half(RANK), edge, 0.0))
    path = None
    paths = []
    for n, edge in enumerate(edges):
        path = edge if path is None else mm(path, jnp.concatenate([edge, edge], axis=0))
        paths.append(path[:, 0:RANK])
    for n in range(levels):
        d[pair_rows(n), :] = jnp.concatenate(
            [records[2 * n, 0:RANK, 0:RANK], records[2 * n + 1, 0:RANK, 0:RANK]], axis=1
        )
    d[pair_rows(levels), :] = top[0:RANK]
    invert_pairs(d, a, m, inv, inv.shape[0] // RANK)
    root_inverse = inv[pair_rows(levels), 0:RANK]
    keep = lax.broadcasted_iota(jnp.int32, (RANK, RANK), 0) >= lax.broadcasted_iota(
        jnp.int32, (RANK, RANK), 1
    )
    root[...] = jnp.where(keep, mm_t(top[0:RANK, 0:RANK], root_inverse), 0.0)
    low = low_half(NRHS)
    xhats = [
        mm_t(
            jnp.where(low, 0.0, swap_halves(records[2 * n + 1, RANK:ROWS])), inv[pair_rows(n), :]
        )
        for n in range(levels)
    ]
    yhats = []
    for n in range(levels):
        pair, half, _ = own_tile(n, grp_count, dev_count, grp_coupling, dev_coupling)
        yhats.append(mm_t(jnp.where(half, twice(xhats[n]), 0.0), pair))
    values = [mm(yhats[n], inv[pair_rows(n), :])[:, 0:RANK] for n in range(levels)]
    value = values[0]
    if levels > 1:
        upper = values[1:]
        if len(upper) % 2:
            upper.append(jnp.zeros_like(value))
            paths.append(jnp.zeros_like(paths[0]))
        value = value + mm_t(jnp.concatenate(upper, axis=1), jnp.concatenate(paths, axis=1))
    value_out[...] = value


def vmem(count):
    return [pl.BlockSpec(memory_space=pltpu.VMEM)] * count


def hbm(count):
    return [pl.BlockSpec(memory_space=pltpu.HBM)] * count


def in_hbm(x):
    return pltpu.with_memory_space_constraint(x, pltpu.HBM)


def f32(*shape):
    return jax.ShapeDtypeStruct(shape, jnp.float32)


def params(mib):
    return pltpu.CompilerParams(vmem_limit_bytes=mib * MIB)


def micros(count):
    return pl.CostEstimate(flops=count * 10**9, bytes_accessed=MIB, transcendentals=0)


def exchange(block, axis, start, bits):
    count = lax.axis_size(axis)
    return [block] + [
        lax.ppermute(block, axis, [(i, i ^ (k << start)) for i in range(count)])
        for k in range(1, 2**bits)
    ]


def chunks(levels, first):
    out = []
    start = 0
    while start < levels:
        bits = min(first if start == 0 else 2, levels - start)
        out.append((start, bits))
        start += bits
    return out


def climb_call(blocks, axis, start, bits, count, transfer, carried=()):
    anywhere = [pl.BlockSpec(memory_space=pl.ANY)] * len(carried)
    return pl.pallas_call(
        functools.partial(climb_kernel, axis, start, bits, count),
        out_shape=[f32(ROWS, RANK), f32(2 * bits, ROWS, PAIR)] + [f32(*c.shape) for c in carried],
        in_specs=vmem(1 + 2**bits) + anywhere,
        out_specs=vmem(2) + anywhere,
        input_output_aliases={1 + 2**bits + n: 2 + n for n in range(len(carried))},
        scratch_shapes=[pltpu.VMEM((2**bits, ROWS, PAIR), jnp.float32)],
        compiler_params=params(8),
        cost_estimate=micros(1),
        name="climb",
    )(transfer, *blocks, *carried)


def local_call(gram, z, rhs, after, near_partner, far_partner):
    return pl.pallas_call(
        local_kernel,
        out_shape=[
            f32(BATCH * RANK, PAIR),
            f32(NRHS, POINT_SPAN + NODE_SPAN),
            jax.ShapeDtypeStruct(near_partner.shape, jnp.int32),
            jax.ShapeDtypeStruct(far_partner.shape, jnp.int32),
        ],
        in_specs=vmem(3) + [pl.BlockSpec(memory_space=pl.ANY)] + hbm(2),
        out_specs=vmem(4),
        scratch_shapes=[
            pltpu.VMEM((RANK, RANK, LANES), jnp.float32),
            pltpu.VMEM((RANK, RANK, LANES), jnp.float32),
            pltpu.SemaphoreType.DMA((2,)),
        ],
        compiler_params=params(24),
        cost_estimate=micros(8),
        name="local_factors",
    )(gram, z, rhs, after, in_hbm(near_partner), in_hbm(far_partner))


def shards(
    rhs,
    leaf_basis,
    near_blocks,
    near_partner,
    local_transfer,
    local_coupling,
    far_partner,
    dev_transfer,
    dev_coupling,
    grp_transfer,
    grp_coupling,
):
    dev_count = lax.axis_size("dev")
    grp_count = lax.axis_size("grp")
    gram, z, top = pl.pallas_call(
        gram_kernel,
        out_shape=[f32(BATCH * RANK, PAIR), f32(NRHS, NODE_SPAN), f32(ROWS, RANK)],
        in_specs=hbm(3),
        out_specs=vmem(3),
        scratch_shapes=[
            pltpu.VMEM((LEAF, POINT_SPAN), jnp.float32),
            pltpu.VMEM((NRHS, POINT_SPAN), jnp.float32),
            pltpu.VMEM((RANK, NODE_SPAN), jnp.float32),
            pltpu.SemaphoreType.DMA((3,)),
        ],
        compiler_params=params(16),
        cost_estimate=micros(4),
        name="gram",
    )(in_hbm(leaf_basis), in_hbm(rhs), in_hbm(local_transfer))

    records = []
    spans = []
    carried = ()
    inv = None
    dev_transfer = dev_transfer[0]
    dev_coupling = dev_coupling[0]
    for start, bits in chunks(dev_count.bit_length() - 1, 1):
        blocks = exchange(top, "dev", start, bits)
        if records and inv is None:
            inv, packed, near_partner, far_partner = local_call(
                gram, z, rhs, records[0], near_partner, far_partner
            )
            carried = (packed,)
        top, record, *carried = climb_call(
            blocks, "dev", start, bits, dev_count, dev_transfer, carried
        )
        records.append(record)
        spans.append(bits)
    packed = carried[0]

    both = ("grp", "dev")
    ends = grp_count * dev_count - 1
    twin = lax.ppermute(packed, both, [(i, i ^ 1) for i in range(ends + 1)])
    pairs = [(i, i + 1) for i in range(1, ends, 2)]
    beside = lax.ppermute(packed, both, pairs + [(j, i) for i, j in pairs])

    grp_chunks = chunks(grp_count.bit_length() - 1, 2)
    levels = sum(spans) + grp_count.bit_length() - 1
    for start, bits in grp_chunks[:-1]:
        blocks = exchange(top, "grp", start, bits)
        top, record = climb_call(blocks, "grp", start, bits, grp_count, grp_transfer)
        records.append(record)
        spans.append(bits)
    start, bits = grp_chunks[-1]
    blocks = exchange(top, "grp", start, bits)
    batch = 8 * ((levels + 1 + 7) // 8)
    value, root = pl.pallas_call(
        functools.partial(top_kernel, grp_count, dev_count, start, bits, tuple(spans)),
        out_shape=[f32(NRHS, RANK), f32(RANK, RANK)],
        in_specs=vmem(4 + len(blocks) + len(records)),
        out_specs=vmem(2),
        scratch_shapes=[
            pltpu.VMEM((2**bits, ROWS, PAIR), jnp.float32),
            pltpu.VMEM((2 * levels, ROWS, PAIR), jnp.float32),
            pltpu.VMEM((batch * RANK, LANES), jnp.float32),
            pltpu.VMEM((RANK, RANK, LANES), jnp.float32),
            pltpu.VMEM((RANK, RANK, LANES), jnp.float32),
            pltpu.VMEM((batch * RANK, PAIR), jnp.float32),
        ],
        compiler_params=params(24),
        cost_estimate=micros(7),
        name="top",
    )(grp_transfer, grp_coupling, dev_transfer, dev_coupling, *blocks, *records)

    window_tiles = 3 * (POINT_SPAN + NODE_SPAN) // PAIR
    product = pl.pallas_call(
        couple_kernel,
        out_shape=f32(NRHS, POINT_SPAN),
        in_specs=[pl.BlockSpec(memory_space=pl.ANY)] * 2 + vmem(9),
        out_specs=vmem(1)[0],
        scratch_shapes=[
            pltpu.VMEM((window_tiles, NRHS, PAIR), jnp.float32),
            pltpu.SMEM(near_partner.shape, jnp.int32),
            pltpu.SMEM(far_partner.shape, jnp.int32),
            pltpu.SemaphoreType.DMA((2,)),
        ],
        compiler_params=params(24),
        cost_estimate=micros(3),
        name="couple",
    )(
        near_partner,
        far_partner,
        packed,
        twin,
        beside,
        inv,
        value,
        local_coupling,
        local_transfer,
        leaf_basis,
        near_blocks,
    )
    return product, root


def solution(mesh):
    return jax.shard_map(
        shards,
        mesh=mesh,
        in_specs=(
            P(None, ("grp", "dev")),
            P(None, ("grp", "dev")),
            P(None, ("grp", "dev")),
            P(("grp", "dev")),
            P(None, ("grp", "dev")),
            P(None, ("grp", "dev")),
            P(("grp", "dev"), None),
            P("grp", None, None),
            P("grp", None, None),
            P(),
            P(),
        ),
        out_specs=(P(None, ("grp", "dev")), P()),
        check_vma=False,
    )
```

```python
import functools

import jax
import jax.numpy as jnp
from jax import lax
from jax.experimental import pallas as pl
from jax.experimental.pallas import tpu as pltpu
from jax.sharding import PartitionSpec as P

RANK = 64
LEAF = 64
NRHS = 16
LOC = 4
LEAF_DEV = 16
LOCAL_NODES = 30
PAIR = 2 * RANK
LANES = 128
BATCH = 16
ROWS = RANK + NRHS
PAIRS = LOCAL_NODES // 2
POINT_SPAN = LEAF_DEV * LEAF
NODE_SPAN = LOCAL_NODES * RANK
OFFSETS = [2 * LEAF_DEV - 2 * (LEAF_DEV >> level) for level in range(LOC)]
MIB = 1 << 20


def halves(x):
    high = x.astype(jnp.bfloat16)
    return high, (x - high.astype(jnp.float32)).astype(jnp.bfloat16)


def three_pass(a, b, side):
    dot = functools.partial(
        lax.dot_general,
        dimension_numbers=(((1,), (side,)), ((), ())),
        preferred_element_type=jnp.float32,
    )
    a_high, a_low = halves(a)
    b_high, b_low = halves(b)
    if a.shape[1] % LANES:
        return dot(a_high, b_high) + (dot(a_high, b_low) + dot(a_low, b_high))
    return dot(
        jnp.concatenate([a_high, a_low, a_high], axis=1),
        jnp.concatenate([b_high, b_high, b_low], axis=side),
    )


def mm(a, b):
    return three_pass(a, b, 0)


def mm_t(a, b):
    return three_pass(a, b, 1)


def gram_pair(u):
    u_high, u_low = halves(u)
    t_high, t_low = halves(u.T)
    dot = functools.partial(jnp.dot, preferred_element_type=jnp.float32)
    wide = dot(t_high, jnp.concatenate([u_high, u_low], axis=1))
    full = wide[:, 0:PAIR] + (wide[:, PAIR:] + dot(t_low, u_high))
    row = lax.broadcasted_iota(jnp.int32, (PAIR, PAIR), 0) < RANK
    return jnp.where(row == low_half(PAIR), full, 0.0)


def low_half(rows):
    return lax.broadcasted_iota(jnp.int32, (rows, PAIR), 1) < RANK


def swap_halves(x):
    return pltpu.roll(x, RANK, 1)


def spread_pair(pair):
    low = low_half(pair.shape[0])
    return jnp.concatenate([jnp.where(low, pair, 0.0), jnp.where(low, 0.0, pair)], axis=0)


def stack_low(pair):
    low = low_half(pair.shape[0])
    return jnp.concatenate(
        [jnp.where(low, pair, 0.0), jnp.where(low, swap_halves(pair), 0.0)], axis=0
    )


def stack_high(pair):
    low = low_half(pair.shape[0])
    return jnp.concatenate(
        [jnp.where(low, 0.0, swap_halves(pair)), jnp.where(low, 0.0, pair)], axis=0
    )


def spaced(tasks, step, steps):
    return tasks[len(tasks) * step // steps : len(tasks) * (step + 1) // steps]


def invert_pairs(gram, a, m, inv, count):
    blocks = RANK // 8
    sub = lax.broadcasted_iota(jnp.int32, (8, LANES), 0)

    def load(i):
        rows = gram[pl.ds(i, count, stride=RANK), :]
        both = jnp.concatenate([rows, swap_halves(rows)], axis=0)
        first = i - i % 8
        a[i, first:RANK, 0 : 2 * count] = both[:, 0:RANK].T[first:]

    def store(i):
        width = i - i % 8 + 8
        rows = m[i, 0:width, 0 : 2 * count].T
        if width < RANK:
            rest = jnp.zeros((2 * count, RANK - width), jnp.float32)
            rows = jnp.concatenate([rows, rest], axis=1)
        inv[pl.ds(i, count, stride=RANK), :] = jnp.concatenate([rows[:count], rows[count:]], axis=1)

    def trail(kb, i):
        k0, first = 8 * kb, i - i % 8
        acc = a[i, first:RANK, :]
        old = m[i, 0:k0, :] if kb else None
        new = None
        for k in range(k0, k0 + 8):
            f = a[k, i : i + 1, :]
            acc = acc - f * a[k, first:RANK, :]
            part = f * m[k, 0 : k0 + 8, :]
            if kb:
                old = old - part[0:k0]
            tail = part[k0 : k0 + 8]
            new = -tail if new is None else new - tail
        a[i, first:RANK, :] = acc
        if kb:
            m[i, 0:k0, :] = old
        m[i, k0 : k0 + 8, :] = new

    for i in range(8):
        load(i)
    tasks = [functools.partial(load, i) for i in range(8, RANK)]
    for kb in range(blocks):
        k0 = 8 * kb
        rows = [a[k0 + k, k0:RANK, :] for k in range(8)]
        mrows = []
        for k in range(8):
            unit = (sub == k).astype(jnp.float32)
            mrows.append(jnp.concatenate([m[k0 + k, 0:k0, :], unit], axis=0) if kb else unit)
        for k in range(8):
            scale = lax.rsqrt(rows[k][k : k + 1, :])
            rows[k] = rows[k] * scale
            mrows[k] = mrows[k] * scale
            for k2 in range(k + 1, 8):
                f = rows[k][k2 : k2 + 1, :]
                rows[k2] = rows[k2] - f * rows[k]
                mrows[k2] = mrows[k2] - f * mrows[k]
            for task in spaced(tasks, k, 8):
                task()
        for k in range(8):
            a[k0 + k, k0:RANK, :] = rows[k]
            m[k0 + k, 0 : k0 + 8, :] = mrows[k]
        stores = [functools.partial(store, i) for i in range(k0, k0 + 8)]
        for i in range(k0 + 8, min(k0 + 16, RANK)):
            trail(kb, i)
        trails = [functools.partial(trail, kb, i) for i in range(k0 + 16, RANK)]
        tasks = []
        for step in range(8):
            tasks += spaced(trails, step, 8) + spaced(stores, step, 8)
    for task in tasks:
        task()


def gram_kernel(basis_in, rhs_in, transfer_in, gram, z_out, top, basis, rhs, transfer, sems):
    copies = [
        pltpu.make_async_copy(source, target, sems.at[n])
        for n, (source, target) in enumerate(
            ((basis_in, basis), (rhs_in, rhs), (transfer_in, transfer))
        )
    ]
    for copy in copies:
        copy.start()
    copies[0].wait()
    copies[1].wait()
    blocks = []
    for p in range(LEAF_DEV // 2):
        u = basis[:, pair_lanes(p)]
        blocks.append(
            jnp.concatenate([gram_pair(u), mm(rhs[:, pair_lanes(p)], spread_pair(u))], axis=0)
        )
    copies[2].wait()
    tile = 0
    low = low_half(RANK)
    for level in range(LOC):
        pairs = len(blocks)
        for p in range(pairs):
            gram[pair_rows(tile + p), :] = jnp.where(
                low, blocks[p][0:RANK], blocks[p][RANK:PAIR]
            )
            z_out[:, pair_lanes(tile + p)] = blocks[p][PAIR:]
        fs = [
            (stack_high if p % 2 else stack_low)(transfer[:, pair_lanes(tile + p)])
            for p in range(pairs)
        ]
        hs = [mm(block, f) for block, f in zip(blocks, fs)]
        parents = []
        for q in range((pairs + 1) // 2):
            both = slice(2 * q, 2 * q + 2)
            g = mm(
                jnp.concatenate([f.T for f in fs[both]], axis=1),
                jnp.concatenate([h[0:PAIR] for h in hs[both]], axis=0),
            )
            parents.append(jnp.concatenate([g, sum(h[PAIR:] for h in hs[both])], axis=0))
        tile += pairs
        blocks = parents
    top[0:RANK, :] = blocks[0][0:RANK, 0:RANK]
    top[RANK:ROWS, :] = blocks[0][PAIR:, 0:RANK]


def pair_rows(p):
    return slice(RANK * p, RANK * (p + 1))


def pair_lanes(p):
    return slice(PAIR * p, PAIR * (p + 1))


def local_kernel(
    gram, z, rhs, after, near_in, far_in, inv, packed, near_partner, far_partner, a, m, sems
):
    copies = [
        pltpu.make_async_copy(near_in, near_partner, sems.at[0]),
        pltpu.make_async_copy(far_in, far_partner, sems.at[1]),
    ]
    for copy in copies:
        copy.start()
    invert_pairs(gram, a, m, inv, BATCH)
    packed[:, 0:POINT_SPAN] = rhs[...]
    for p in range(PAIRS):
        packed[:, POINT_SPAN + PAIR * p : POINT_SPAN + PAIR * (p + 1)] = mm_t(
            z[:, pair_lanes(p)], spread_pair(inv[pair_rows(p), :])
        )
    for copy in copies:
        copy.wait()


def merge(nodes, tile, transfer):
    pairs = range(len(nodes) // 2)
    fs = [
        stack_low(transfer[:, pl.ds(pl.multiple_of(PAIR * (tile + p), PAIR), PAIR)]) for p in pairs
    ]
    hs = [
        mm(jnp.concatenate([nodes[2 * p], swap_halves(nodes[2 * p + 1])], axis=0), fs[p])
        for p in pairs
    ]
    gs = [
        mm(f[:, 0:RANK].T, jnp.concatenate([h[0:RANK], h[ROWS : ROWS + RANK]], axis=0))
        for f, h in zip(fs, hs)
    ]
    return [
        jnp.concatenate([g, h[RANK:ROWS] + h[ROWS + RANK :]], axis=0) for g, h in zip(gs, hs)
    ]


def climb(blocks, place, start, bits, count, transfer, stack, records, first_record):
    empty = jnp.zeros((ROWS, RANK), jnp.float32)
    for k, block in enumerate(blocks):
        stack[k] = jnp.concatenate([block[...], empty], axis=1)
    here = lax.shift_right_logical(place, start)
    low = here & (2**bits - 1)
    base = here - low
    nodes = [stack[c ^ low] for c in range(2**bits)]
    for level in range(start, start + bits):
        m = count >> level
        own, sibling = (0, 1) if level == start else (low, low ^ 1)
        records[2 * (first_record + level - start)] = stack[own]
        records[2 * (first_record + level - start) + 1] = stack[sibling]
        tile = (2 * count - 2 * m + base) // 2
        nodes = merge(nodes, tile, transfer)
        low = lax.shift_right_logical(low, 1)
        base = lax.shift_right_logical(base, 1)
        for c, node in enumerate(nodes):
            stack[c] = node
    return nodes[0]


def climb_kernel(axis, start, bits, count, transfer, *refs):
    blocks = refs[: 2**bits]
    top, records = refs[-3 - (len(refs) - 2**bits - 3) // 2 :][:2]
    stack = refs[-1]
    top[...] = climb(blocks, lax.axis_index(axis), start, bits, count, transfer, stack, records, 0)[
        :, 0:RANK
    ]


def own_tile(n, grp_count, dev_count, grp_blocks, dev_blocks):
    dev_levels = dev_count.bit_length() - 1
    if n < dev_levels:
        count, shift, place, blocks = dev_count, n, lax.axis_index("dev"), dev_blocks
    else:
        count, shift, place, blocks = grp_count, n - dev_levels, lax.axis_index("grp"), grp_blocks
    index = 2 * count - 2 * (count >> shift) + lax.shift_right_logical(place, shift)
    pair = blocks[:, pl.ds(pl.multiple_of(PAIR * (index // 2), PAIR), PAIR)]
    lane = lax.broadcasted_iota(jnp.int32, (NRHS, PAIR), 1)
    odd = index % 2
    return pair, lax.shift_right_logical(lane, RANK.bit_length() - 1) == odd, odd == 1


def couple_kernel(
    near_partner_in,
    far_partner_in,
    own,
    twin,
    beside,
    inv,
    root_value,
    coupling,
    transfer,
    basis,
    near,
    product,
    window,
    near_partner,
    far_partner,
    sems,
):
    copies = [
        pltpu.make_async_copy(near_partner_in, near_partner, sems.at[0]),
        pltpu.make_async_copy(far_partner_in, far_partner, sems.at[1]),
    ]
    for copy in copies:
        copy.start()
    packed_tiles = (POINT_SPAN + NODE_SPAN) // PAIR
    point_tiles = POINT_SPAN // PAIR
    starts = [point_tiles + OFFSETS[level] // 2 for level in range(LOC)]
    spans = [(0, point_tiles)] + [(starts[level], (LEAF_DEV >> level) // 2) for level in range(LOC)]
    firsts = []
    slot = 0
    place = lax.axis_index("grp") * lax.axis_size("dev") + lax.axis_index("dev")
    odd = place & 1
    for start, span in spans:
        firsts.append(slot)
        for source, shift in ((beside, odd), (own, None), (twin, 1 - odd)):
            first = slot + span if shift is None else slot + 2 * span * shift
            for t in range(span):
                tile = source[:, PAIR * (start + t) : PAIR * (start + t + 1)]
                window[first + t] = tile
        slot += 3 * span

    def pick(first, index, parity):
        tile = window[first + lax.shift_right_logical(index, 1)]
        return jnp.where((index & 1) == parity, tile, swap_halves(tile))

    low16 = low_half(NRHS)
    for copy in copies:
        copy.wait()
    coupled = []
    for level in range(LOC):
        m = LEAF_DEV >> level
        for p in range(m // 2):
            node = OFFSETS[level] + 2 * p
            values = []
            for side in range(2):
                index = far_partner[0, node + side] - (place - 1) * m
                values.append(pick(firsts[level + 1], index, side))
            xhat = jnp.where(low16, values[0], values[1])
            coupled.append(mm_t(xhat, spread_pair(coupling[:, pair_lanes(node // 2)])))

    def terms(level):
        tile = OFFSETS[level] // 2
        return [
            mm(coupled[p], spread_pair(inv[pair_rows(p), :]))
            for p in range(tile, tile + (LEAF_DEV >> level + 1))
        ]

    def near_field(p):
        own_points = own[:, pair_lanes(p)]
        swapped = swap_halves(own_points)
        inputs = []
        for side in range(2):
            index = near_partner[2 * p + side] - (place - 1) * LEAF_DEV
            partner = pick(0, index, 1)
            inputs.append(jnp.where(low16, swapped if side else own_points, partner))
        weights = jnp.concatenate(
            [
                near[:, 2 * PAIR * p : 2 * PAIR * p + PAIR],
                near[:, 2 * PAIR * p + PAIR : 2 * PAIR * (p + 1)],
            ],
            axis=0,
        )
        out = mm_t(jnp.concatenate(inputs, axis=0), weights)
        return jnp.where(low16, out[0:NRHS], out[NRHS:])

    nears = []
    state = [twice(root_value[...])]
    ready = terms(LOC - 1)
    for level in reversed(range(LOC)):
        tile = OFFSETS[level] // 2
        pairs = LEAF_DEV >> level + 1
        swept = [
            mm_t(
                state[p // 2],
                (stack_high if p % 2 else stack_low)(transfer[:, pair_lanes(tile + p)]),
            )
            for p in range(pairs)
        ]
        state = [term + value for term, value in zip(ready, swept)]
        if level:
            ready = terms(level - 1)
        nears += [near_field(p) for p in range(2 * len(nears) // 2, 2 * (LOC - level))]
    for p in range(LEAF_DEV // 2):
        product[:, pair_lanes(p)] = nears[p] + mm_t(
            state[p], spread_pair(basis[:, pair_lanes(p)])
        )


def twice(x):
    return jnp.concatenate([x, x], axis=1)


def top_kernel(
    grp_count,
    dev_count,
    start,
    bits,
    record_spans,
    grp_transfer,
    grp_coupling,
    dev_transfer,
    dev_coupling,
    *refs,
):
    blocks = refs[: 2**bits]
    refs = refs[2**bits :]
    earlier = refs[: len(record_spans)]
    value_out, root, stack, records, d, a, m, inv = refs[len(record_spans) :]
    level = 0
    for ref, span in zip(earlier, record_spans):
        for r in range(2 * span):
            records[2 * level + r] = ref[r]
        level += span
    top = climb(
        blocks, lax.axis_index("grp"), start, bits, grp_count, grp_transfer, stack, records, level
    )
    levels = level + bits
    edges = []
    for n in range(levels - 1):
        pair, _, odd_node = own_tile(n, grp_count, dev_count, grp_transfer, dev_transfer)
        edge = jnp.where(odd_node, swap_halves(pair), pair)
        edges.append(jnp.where(low_half(RANK), edge, 0.0))
    path = None
    paths = []
    for n, edge in enumerate(edges):
        path = edge if path is None else mm(path, jnp.concatenate([edge, edge], axis=0))
        paths.append(path[:, 0:RANK])
    for n in range(levels):
        d[pair_rows(n), :] = jnp.concatenate(
            [records[2 * n, 0:RANK, 0:RANK], records[2 * n + 1, 0:RANK, 0:RANK]], axis=1
        )
    d[pair_rows(levels), :] = top[0:RANK]
    invert_pairs(d, a, m, inv, inv.shape[0] // RANK)
    root_inverse = inv[pair_rows(levels), 0:RANK]
    keep = lax.broadcasted_iota(jnp.int32, (RANK, RANK), 0) >= lax.broadcasted_iota(
        jnp.int32, (RANK, RANK), 1
    )
    root[...] = jnp.where(keep, mm_t(top[0:RANK, 0:RANK], root_inverse), 0.0)
    low = low_half(NRHS)
    xhats = [
        mm_t(
            jnp.where(low, 0.0, swap_halves(records[2 * n + 1, RANK:ROWS])), inv[pair_rows(n), :]
        )
        for n in range(levels)
    ]
    yhats = []
    for n in range(levels):
        pair, half, _ = own_tile(n, grp_count, dev_count, grp_coupling, dev_coupling)
        yhats.append(mm_t(jnp.where(half, twice(xhats[n]), 0.0), pair))
    values = [mm(yhats[n], inv[pair_rows(n), :])[:, 0:RANK] for n in range(levels)]
    value = values[0]
    if levels > 1:
        upper = values[1:]
        if len(upper) % 2:
            upper.append(jnp.zeros_like(value))
            paths.append(jnp.zeros_like(paths[0]))
        value = value + mm_t(jnp.concatenate(upper, axis=1), jnp.concatenate(paths, axis=1))
    value_out[...] = value


def vmem(count):
    return [pl.BlockSpec(memory_space=pltpu.VMEM)] * count


def hbm(count):
    return [pl.BlockSpec(memory_space=pltpu.HBM)] * count


def in_hbm(x):
    return pltpu.with_memory_space_constraint(x, pltpu.HBM)


def f32(*shape):
    return jax.ShapeDtypeStruct(shape, jnp.float32)


def params(mib):
    return pltpu.CompilerParams(vmem_limit_bytes=mib * MIB)


def micros(count):
    return pl.CostEstimate(flops=count * 10**9, bytes_accessed=MIB, transcendentals=0)


def exchange(block, axis, start, bits):
    count = lax.axis_size(axis)
    return [block] + [
        lax.ppermute(block, axis, [(i, i ^ (k << start)) for i in range(count)])
        for k in range(1, 2**bits)
    ]


def chunks(levels, first):
    out = []
    start = 0
    while start < levels:
        bits = min(first if start == 0 else 2, levels - start)
        out.append((start, bits))
        start += bits
    return out


def climb_call(blocks, axis, start, bits, count, transfer, carried=()):
    anywhere = [pl.BlockSpec(memory_space=pl.ANY)] * len(carried)
    return pl.pallas_call(
        functools.partial(climb_kernel, axis, start, bits, count),
        out_shape=[f32(ROWS, RANK), f32(2 * bits, ROWS, PAIR)] + [f32(*c.shape) for c in carried],
        in_specs=vmem(1 + 2**bits) + anywhere,
        out_specs=vmem(2) + anywhere,
        input_output_aliases={1 + 2**bits + n: 2 + n for n in range(len(carried))},
        scratch_shapes=[pltpu.VMEM((2**bits, ROWS, PAIR), jnp.float32)],
        compiler_params=params(8),
        cost_estimate=micros(1),
        name="climb",
    )(transfer, *blocks, *carried)


def local_call(gram, z, rhs, after, near_partner, far_partner):
    return pl.pallas_call(
        local_kernel,
        out_shape=[
            f32(BATCH * RANK, PAIR),
            f32(NRHS, POINT_SPAN + NODE_SPAN),
            jax.ShapeDtypeStruct(near_partner.shape, jnp.int32),
            jax.ShapeDtypeStruct(far_partner.shape, jnp.int32),
        ],
        in_specs=vmem(3) + [pl.BlockSpec(memory_space=pl.ANY)] + hbm(2),
        out_specs=vmem(4),
        scratch_shapes=[
            pltpu.VMEM((RANK, RANK, LANES), jnp.float32),
            pltpu.VMEM((RANK, RANK, LANES), jnp.float32),
            pltpu.SemaphoreType.DMA((2,)),
        ],
        compiler_params=params(24),
        cost_estimate=micros(8),
        name="local_factors",
    )(gram, z, rhs, after, in_hbm(near_partner), in_hbm(far_partner))


def shards(
    rhs,
    leaf_basis,
    near_blocks,
    near_partner,
    local_transfer,
    local_coupling,
    far_partner,
    dev_transfer,
    dev_coupling,
    grp_transfer,
    grp_coupling,
):
    dev_count = lax.axis_size("dev")
    grp_count = lax.axis_size("grp")
    gram, z, top = pl.pallas_call(
        gram_kernel,
        out_shape=[f32(BATCH * RANK, PAIR), f32(NRHS, NODE_SPAN), f32(ROWS, RANK)],
        in_specs=hbm(3),
        out_specs=vmem(3),
        scratch_shapes=[
            pltpu.VMEM((LEAF, POINT_SPAN), jnp.float32),
            pltpu.VMEM((NRHS, POINT_SPAN), jnp.float32),
            pltpu.VMEM((RANK, NODE_SPAN), jnp.float32),
            pltpu.SemaphoreType.DMA((3,)),
        ],
        compiler_params=params(16),
        cost_estimate=micros(4),
        name="gram",
    )(in_hbm(leaf_basis), in_hbm(rhs), in_hbm(local_transfer))

    records = []
    spans = []
    carried = ()
    inv = None
    dev_transfer = dev_transfer[0]
    dev_coupling = dev_coupling[0]
    for start, bits in chunks(dev_count.bit_length() - 1, 1):
        blocks = exchange(top, "dev", start, bits)
        if records and inv is None:
            inv, packed, near_partner, far_partner = local_call(
                gram, z, rhs, records[0], near_partner, far_partner
            )
            carried = (packed,)
        top, record, *carried = climb_call(
            blocks, "dev", start, bits, dev_count, dev_transfer, carried
        )
        records.append(record)
        spans.append(bits)
    packed = carried[0]

    both = ("grp", "dev")
    ends = grp_count * dev_count - 1
    twin = lax.ppermute(packed, both, [(i, i ^ 1) for i in range(ends + 1)])
    pairs = [(i, i + 1) for i in range(1, ends, 2)]
    beside = lax.ppermute(packed, both, pairs + [(j, i) for i, j in pairs])

    grp_chunks = chunks(grp_count.bit_length() - 1, 2)
    levels = sum(spans) + grp_count.bit_length() - 1
    for start, bits in grp_chunks[:-1]:
        blocks = exchange(top, "grp", start, bits)
        top, record = climb_call(blocks, "grp", start, bits, grp_count, grp_transfer)
        records.append(record)
        spans.append(bits)
    start, bits = grp_chunks[-1]
    blocks = exchange(top, "grp", start, bits)
    batch = 8 * ((levels + 1 + 7) // 8)
    value, root = pl.pallas_call(
        functools.partial(top_kernel, grp_count, dev_count, start, bits, tuple(spans)),
        out_shape=[f32(NRHS, RANK), f32(RANK, RANK)],
        in_specs=vmem(4 + len(blocks) + len(records)),
        out_specs=vmem(2),
        scratch_shapes=[
            pltpu.VMEM((2**bits, ROWS, PAIR), jnp.float32),
            pltpu.VMEM((2 * levels, ROWS, PAIR), jnp.float32),
            pltpu.VMEM((batch * RANK, LANES), jnp.float32),
            pltpu.VMEM((RANK, RANK, LANES), jnp.float32),
            pltpu.VMEM((RANK, RANK, LANES), jnp.float32),
            pltpu.VMEM((batch * RANK, PAIR), jnp.float32),
        ],
        compiler_params=params(24),
        cost_estimate=micros(7),
        name="top",
    )(grp_transfer, grp_coupling, dev_transfer, dev_coupling, *blocks, *records)

    window_tiles = 3 * (POINT_SPAN + NODE_SPAN) // PAIR
    product = pl.pallas_call(
        couple_kernel,
        out_shape=f32(NRHS, POINT_SPAN),
        in_specs=[pl.BlockSpec(memory_space=pl.ANY)] * 2 + vmem(9),
        out_specs=vmem(1)[0],
        scratch_shapes=[
            pltpu.VMEM((window_tiles, NRHS, PAIR), jnp.float32),
            pltpu.SMEM(near_partner.shape, jnp.int32),
            pltpu.SMEM(far_partner.shape, jnp.int32),
            pltpu.SemaphoreType.DMA((2,)),
        ],
        compiler_params=params(24),
        cost_estimate=micros(3),
        name="couple",
    )(
        near_partner,
        far_partner,
        packed,
        twin,
        beside,
        inv,
        value,
        local_coupling,
        local_transfer,
        leaf_basis,
        near_blocks,
    )
    return product, root


def solution(mesh):
    return jax.shard_map(
        shards,
        mesh=mesh,
        in_specs=(
            P(None, ("grp", "dev")),
            P(None, ("grp", "dev")),
            P(None, ("grp", "dev")),
            P(("grp", "dev")),
            P(None, ("grp", "dev")),
            P(None, ("grp", "dev")),
            P(("grp", "dev"), None),
            P("grp", None, None),
            P("grp", None, None),
            P(),
            P(),
        ),
        out_specs=(P(None, ("grp", "dev")), P()),
        check_vma=False,
    )
```
